256 devices in a mesh: tile: 16 (over x, z_lo, core), kern: 16 (over y, z_hi).
Axes of the slice: x: 4, y: 4, z: 8 (z_hi: 4, z_lo: 2; z = z_hi * 2 + z_lo), core: 2. Of those that a mesh axis runs over, the one named last changes fastest.
Arguments:
- mask_field: float32 [4096, 1024], P('tile', 'kern'), may hold values from -6 to 6
- target: int32 [4096, 1024], P('tile'), may hold values 0 or 1
- kernel_spectra: float32 [32, 2, 128, 128], P('kern'), may hold values from -5 to 5
- kernel_weight: float32 [32], P('kern'), may hold values from 0.01 to 0.1
Outputs:
- resist: float32 [4096, 1024], P('tile', 'kern')
- mask_grad: float32 [4096, 1024], P('tile', 'kern')
The draws below stay inside these ranges and needn't reach their ends.
All inputs are finite; a program needn't handle non-finite values. No bound on the sum of `target` on one device may be relied on, other than what follows from the above.
Results may differ from the reference program's by a relative error of at most 0.00065.
Values may be sent and summed in bfloat16 or wider, within the bound.
No kernel may reach another device: no remote copies, remote signals or barrier semaphores. Data moves between devices by JAX's collectives and lax.ppermute only.
A program may use at most 64 MiB of HBM per device.

```python
import math
import jax
import jax.numpy as jnp
from jax import lax

MASK_COLS = 1024
HALO_ROWS = 128
ROW_FREQS = 128
COL_FREQS = 128
TILE_ROWS = 256
KERNELS = 32
STRIP_ROWS = 4096
WINDOW = 512


def set_ends(array, rng, low, top_value):
    index_at = [jax.random.randint(jax.random.fold_in(rng, axis), (), 0, length) for axis, length in enumerate(array.shape)]
    widest = array.shape.index(max(array.shape))
    neighbour = index_at[:widest] + [(index_at[widest] + 1) % array.shape[widest]] + index_at[widest + 1:]
    return array.at[tuple(index_at)].set(low).at[tuple(neighbour)].set(top_value)


def block_scale(rng, shape, shards, smallest, top_value):
    level, own = 1.0, jax.random.fold_in(rng, 6)
    for dim, blocks in shards:
        heights = jnp.exp(jax.random.uniform(jax.random.fold_in(own, dim), (blocks,), jnp.float32, smallest / len(shards), top_value / len(shards)))
        level = level * jnp.repeat(heights, shape[dim] // blocks).reshape([-1 if axis == dim else 1 for axis in range(len(shape))])
    return level


def gaussian(key, dims, width, bound, shards=(), kind=jnp.bfloat16):
    array = jax.random.normal(key, dims, jnp.float32) * width
    if len(shards) > 0:
        array = block_scale(key, dims, shards, -0.22, 0.18) * array
    return jnp.clip(array, min=-bound, max=bound).astype(kind)


def setup_inputs(seed: int = 0) -> dict:
    streams_of = jax.random.split(jax.random.key(seed), 5)
    mask_field = gaussian(streams_of[0], (STRIP_ROWS, MASK_COLS), 1.0, 6.0, ((0, 16), (1, 16)), jnp.float32)
    target = set_ends((jax.random.randint(streams_of[1], (STRIP_ROWS, MASK_COLS), 0, 2) < 1).astype(jnp.int32), jax.random.fold_in(streams_of[1], 1), 0, 1)
    kernel_spectra = gaussian(streams_of[2], (KERNELS, 2, ROW_FREQS, COL_FREQS), 0.7071, 5.0, ((0, 16),), jnp.float32)
    kernel_weight = jnp.clip(jnp.exp(math.log(0.1) - 2.3025851 * jax.random.uniform(streams_of[3], (KERNELS,), jnp.float32) ** block_scale(streams_of[3], (KERNELS,), ((0, 16),), -0.2, 0.2)), 0.01, 0.1)
    return {"mask_field": mask_field, "target": target, "kernel_spectra": kernel_spectra, "kernel_weight": kernel_weight}


STEEPNESS = 4.0
THRESHOLD = 1.0


def band_index(count, length):
    return (jnp.arange(count, dtype=jnp.int32) - count // 2) % length


def reference(mask_field, target, kernel_spectra, kernel_weight):
    tile_count = STRIP_ROWS // TILE_ROWS
    padded = jnp.pad(mask_field, ((HALO_ROWS, HALO_ROWS), (0, 0)))
    row_index = band_index(ROW_FREQS, WINDOW)
    col_index = band_index(COL_FREQS, MASK_COLS)
    full_scale = 1.0 / (WINDOW * MASK_COLS) ** 0.5
    band_scale = 1.0 / (ROW_FREQS * COL_FREQS) ** 0.5
    kernels = kernel_spectra[:, 0] + 1j * kernel_spectra[:, 1]

    def to_grid(values):
        grid = jnp.zeros((WINDOW, MASK_COLS), values.dtype)
        return grid.at[row_index[:, None], col_index[None, :]].set(values)

    def in_band(values):
        return values[row_index][:, col_index]

    def one_tile(tile_index):
        window = lax.dynamic_slice_in_dim(padded, tile_index * TILE_ROWS, WINDOW, 0)
        spectrum = in_band(jnp.fft.fft2(window)) * full_scale
        target_tile = lax.dynamic_slice_in_dim(target, tile_index * TILE_ROWS, TILE_ROWS, 0).astype(jnp.float32)

        def amplitude(kernel):
            aerial = jnp.fft.ifft2(to_grid(kernel * spectrum)) * (WINDOW * MASK_COLS * band_scale)
            return aerial[HALO_ROWS:HALO_ROWS + TILE_ROWS]

        def add_image(running, member):
            kernel, weight = member
            aerial = amplitude(kernel)
            return running + weight * (aerial.real ** 2 + aerial.imag ** 2), None

        intensity, unused = lax.scan(add_image, jnp.zeros((TILE_ROWS, MASK_COLS), jnp.float32), (kernels, kernel_weight))
        resist = jax.nn.sigmoid(STEEPNESS * (intensity - THRESHOLD))
        slope_map = (2.0 * STEEPNESS) * (resist - target_tile) * resist * (1.0 - resist)
        slope_map = lax.optimization_barrier(slope_map.astype(jnp.bfloat16)).astype(jnp.float32)

        def add_slope(running, member):
            kernel, weight = member
            aerial = amplitude(kernel)
            placed = jnp.zeros((WINDOW, MASK_COLS), aerial.dtype).at[HALO_ROWS:HALO_ROWS + TILE_ROWS].set(slope_map * jnp.conj(aerial))
            adjoint = in_band(jnp.fft.ifft2(placed)) * (WINDOW * MASK_COLS * band_scale)
            return running + weight * kernel * adjoint, None

        combined, unused = lax.scan(add_slope, jnp.zeros((ROW_FREQS, COL_FREQS), spectrum.dtype), (kernels, kernel_weight))
        window_grad = (2.0 * full_scale) * jnp.fft.fft2(to_grid(combined)).real
        return resist, window_grad

    resists, windows = lax.map(one_tile, jnp.arange(tile_count, dtype=jnp.int32))
    core = windows[:, HALO_ROWS:HALO_ROWS + TILE_ROWS]
    edge_zero = jnp.zeros((1, HALO_ROWS, MASK_COLS), jnp.float32)
    from_above = jnp.concatenate([edge_zero, windows[:-1, HALO_ROWS + TILE_ROWS:]], 0)
    from_below = jnp.concatenate([windows[1:, :HALO_ROWS], edge_zero], 0)
    core = core.at[:, :HALO_ROWS].add(from_above)
    core = core.at[:, TILE_ROWS - HALO_ROWS:].add(from_below)
    return resists.reshape(STRIP_ROWS, MASK_COLS), core.reshape(STRIP_ROWS, MASK_COLS)
```

```python
import math

import jax
import jax.numpy as jnp
import numpy as np
from jax import lax
from jax.sharding import PartitionSpec as P

COLS = 1024
HALO = 128
FREQS = 128
TILE = 256
WINDOW = 512
SIDE = 4
SHARD = 64
SAMPLES = 256
QUARTER = 64
STEEPNESS = 4.0
THRESHOLD = 1.0

HIGH = lax.Precision.HIGHEST


def angles(places, frequencies, length):
    return (np.outer(places, frequencies) % length) * (2.0 * math.pi / length)


def tables():
    freq = np.arange(FREQS) - FREQS // 2
    scale = 1.0 / math.sqrt(WINDOW * COLS)
    win = angles(freq, np.arange(WINDOW), WINDOW)
    row_cos = np.cos(win) * scale
    row_sin = -np.sin(win) * scale
    col = angles(np.arange(COLS), freq, COLS)
    cos, sin = np.cos(col), np.sin(col)
    cos = cos.reshape(COLS // SHARD, SHARD, FREQS)
    sin = sin.reshape(COLS // SHARD, SHARD, FREQS)
    band = np.concatenate(
        [np.concatenate([cos, -sin], 2), np.concatenate([sin, cos], 2)], 1
    )
    out = angles(HALO + np.arange(TILE), freq, WINDOW)
    out_cos, out_sin = np.cos(out), np.sin(out)
    pix = angles(freq, np.arange(SAMPLES), SAMPLES)
    pix_cos, pix_sin = np.cos(pix), np.sin(pix)
    pixels = np.concatenate(
        [np.concatenate([pix_cos, pix_sin], 1), np.concatenate([-pix_sin, pix_cos], 1)], 0
    )
    gap = np.arange(COLS)[None, :] - (COLS // SAMPLES) * np.arange(SAMPLES)[:, None]
    waves = np.arange(1, SAMPLES // 2)
    base = 2.0 * math.pi / COLS
    line = (1.0 + 2.0 * np.cos(base * np.outer(np.arange(COLS), waves)).sum(1)) / SAMPLES
    spread = line[gap % COLS]
    as32 = lambda value: value.astype(np.float32)
    return tuple(
        map(as32, (row_cos, row_sin, band, np.concatenate([out_cos, out_sin], 1), pixels, spread))
    )


def dot(former, latter, dims=((1,), (0,))):
    return lax.dot_general(
        former, latter, (dims, ((), ())), precision=HIGH, preferred_element_type=jnp.float32
    )


def shift_y(value, step):
    route = [(4 * y + z, 4 * ((y + step) % 4) + z) for y in range(4) for z in range(4)]
    return lax.ppermute(value, "kern", route)


def shift_z(value, step):
    route = [(4 * y + z, 4 * y + (z + step) % 4) for y in range(4) for z in range(4)]
    return lax.ppermute(value, "kern", route)


def shift_tile(value, step):
    peers = lax.axis_size("tile")
    return lax.ppermute(value, "tile", [(i, (i + step) % peers) for i in range(peers)])


def swap_core(value):
    return lax.ppermute(value, "tile", [(i, i ^ 1) for i in range(lax.axis_size("tile"))])


def sum_over(value, shift):
    return value + shift(value, 1) + shift(value, 2) + shift(value, 3)


def per_device(mask_field, target, kernel_spectra, kernel_weight):
    row_cos, row_sin, band, out_table, pixels, spread = tables()
    tile = lax.axis_index("tile")
    kern = lax.axis_index("kern")
    at_y, at_z = kern // 4, kern % 4
    core = tile % 2
    above = shift_tile(mask_field[TILE - HALO :], 1)
    below = shift_tile(mask_field[:HALO], -1)

    scaled = kernel_spectra * (jnp.sqrt(kernel_weight) / FREQS)[:, None, None, None]
    own_half = lax.dynamic_index_in_dim(scaled, core, 0, False)
    half = jnp.stack([own_half] + [shift_y(own_half, step) for step in (1, 2, 3)])
    kernels = jnp.concatenate([half, swap_core(half)], 0)

    above = jnp.where(tile > 0, above, 0.0)
    below = jnp.where(tile < lax.axis_size("tile") - 1, below, 0.0)
    window = jnp.concatenate([above, mask_field, below], 0)
    rows_done = jnp.concatenate([dot(row_cos, window), dot(row_sin, window)], 1)

    band_of = lambda step: lax.dynamic_index_in_dim(
        band, 4 * at_y + (at_z + step) % 4, 0, False
    )
    bands = [band_of(step) for step in range(4)]
    part = dot(rows_done, bands[0])
    for step in (1, 2, 3):
        part = part + dot(shift_z(rows_done, -step), bands[step])
    spectrum = sum_over(part, shift_y)
    spec_re, spec_im = spectrum[:, :FREQS], spectrum[:, FREQS:]

    out_rows = lax.dynamic_slice_in_dim(out_table, at_y * QUARTER, QUARTER, 0)
    out_re, out_im = out_rows[:, :FREQS], out_rows[:, FREQS:]
    count = kernels.shape[0]
    fields = []
    image = jnp.zeros((QUARTER, SAMPLES), jnp.float32)
    for slot in range(count):
        kern_re, kern_im = kernels[slot, 0], kernels[slot, 1]
        band_re = kern_re * spec_re - kern_im * spec_im
        band_im = kern_re * spec_im + kern_im * spec_re
        block = jnp.concatenate(
            [jnp.concatenate([band_re, band_im], 1), jnp.concatenate([-band_im, band_re], 1)], 0
        )
        field = dot(dot(out_rows, block), pixels)
        fields.append(field)
        image = image + field[:, :SAMPLES] ** 2 + field[:, SAMPLES:] ** 2
    image = dot(sum_over(image, shift_z), spread)
    resist = jax.nn.sigmoid(STEEPNESS * (image - THRESHOLD))
    goal = lax.dynamic_slice_in_dim(target, at_y * QUARTER, QUARTER, 0).astype(jnp.float32)
    slope = 2.0 * STEEPNESS * (resist - goal) * resist * (1.0 - resist)
    slope = slope.astype(jnp.bfloat16).astype(jnp.float32)
    slope = dot(slope, spread, ((1,), (1,)))

    grad_re = jnp.zeros((FREQS, FREQS), jnp.float32)
    grad_im = jnp.zeros((FREQS, FREQS), jnp.float32)
    back_rows = jnp.concatenate([out_re, out_im], 0)
    for slot in range(count):
        kern_re, kern_im = kernels[slot, 0], kernels[slot, 1]
        weighted = jnp.concatenate([slope, slope], 1) * fields[slot]
        freqs = dot(weighted, pixels, ((1,), (1,)))
        turned = jnp.concatenate([freqs[:, FREQS:], -freqs[:, :FREQS]], 1)
        adjoint = dot(back_rows, jnp.concatenate([freqs, turned], 0), ((0,), (0,)))
        adj_re, adj_im = adjoint[:, :FREQS], adjoint[:, FREQS:]
        grad_re = grad_re + kern_re * adj_re + kern_im * adj_im
        grad_im = grad_im + kern_re * adj_im - kern_im * adj_re
    grad = sum_over(jnp.concatenate([grad_re, grad_im], 1), shift_y)

    column_parts = [dot(grad, bands[step], ((1,), (1,))) for step in range(4)]
    rows_grad = column_parts[0]
    for step in (1, 2, 3):
        rows_grad = rows_grad + shift_z(column_parts[step], step)
    grad_re, grad_im = rows_grad[:, :SHARD], rows_grad[:, SHARD:]
    window_grad = 2.0 * (
        dot(row_cos, grad_re, ((0,), (0,))) + dot(row_sin, grad_im, ((0,), (0,)))
    )
    from_above = shift_tile(window_grad[WINDOW - HALO :], 1)
    from_below = shift_tile(window_grad[:HALO], -1)
    from_above = jnp.where(tile > 0, from_above, 0.0)
    from_below = jnp.where(tile < lax.axis_size("tile") - 1, from_below, 0.0)
    mask_grad = window_grad[HALO : HALO + TILE] + jnp.concatenate([from_above, from_below], 0)

    place = lambda step: lax.dynamic_slice_in_dim(
        resist, (4 * ((at_y + step) % 4) + at_z) * SHARD, SHARD, 1
    )
    pieces = [place(0)] + [shift_y(place(step), step) for step in (1, 2, 3)]
    resist_own = jnp.zeros((TILE, SHARD), jnp.float32)
    for step in range(4):
        resist_own = lax.dynamic_update_slice_in_dim(
            resist_own, pieces[step], ((at_y - step) % 4) * QUARTER, 0
        )
    return (resist_own, mask_grad)


def solution(mesh):
    in_specs = (P("tile", "kern"), P("tile", None), P("kern", None, None, None), P("kern"))
    out_specs = (P("tile", "kern"), P("tile", "kern"))
    return jax.shard_map(
        per_device, mesh=mesh, in_specs=in_specs, out_specs=out_specs, check_vma=False
    )
```

```python
import math

import jax
import jax.numpy as jnp
import ml_dtypes
import numpy as np
from jax import lax
from jax.experimental import pallas as pl
from jax.experimental.pallas import tpu as pltpu
from jax.sharding import PartitionSpec as P

COLS = 1024
HALO = 128
FREQS = 128
TILE = 256
WINDOW = 512
SHARD = 64
SAMPLES = 256
QUARTER = 64
COUNT = 8
HALF = 72
EDGE_ROW = 65
WEIGHT_ROW = 67
EXTRA = 32
WIDE = 4 * SHARD
STEEPNESS = 4.0
THRESHOLD = 1.0
F32 = jnp.float32
BF16 = jnp.bfloat16


def angles(places, frequencies, length):
    return (np.outer(places, frequencies) % length) * (2.0 * math.pi / length)


def split_table(value):
    value = value.astype(np.float32)
    high = value.astype(ml_dtypes.bfloat16)
    low = (value - high.astype(np.float32)).astype(ml_dtypes.bfloat16)
    return np.stack([high, low])


def tables():
    freq = np.arange(FREQS) - FREQS // 2
    scale = 1.0 / math.sqrt(WINDOW * COLS)
    win = angles(np.arange(FREQS // 2 + 1), np.arange(WINDOW), WINDOW)
    rows = np.zeros((2, HALF, WINDOW))
    rows[0, : FREQS // 2 + 1] = np.cos(win) * scale
    rows[1, : FREQS // 2 + 1] = np.sin(win) * scale
    rows = rows.reshape(2 * HALF, WINDOW)
    col = angles(np.arange(COLS), freq, COLS)
    keep = FREQS // 2
    band = np.concatenate([np.cos(col[:, keep:]), np.sin(col[:, keep:])], 1)
    band[:, keep] = np.cos(col[:, 0])
    edge = np.zeros((16, COLS))
    edge[0] = np.sin(col[:, 0])
    unfold = np.zeros((FREQS, 2 * FREQS))
    for place, value in enumerate(freq):
        size = abs(value)
        unfold[size, place] = 1.0
        if 0 < size < keep:
            unfold[keep + size, FREQS + place] = np.sign(value)
    flip = np.zeros((FREQS // 2, HALF))
    flip[np.arange(FREQS // 2), FREQS // 2 - np.arange(FREQS // 2)] = 1.0
    out = angles(HALO + np.arange(TILE), freq, WINDOW).reshape(4, QUARTER, FREQS)
    out_rows = np.concatenate([np.cos(out), np.sin(out)], 1) / FREQS
    pix = angles(freq, np.arange(SAMPLES), SAMPLES)
    pix_cos, pix_sin = np.cos(pix), np.sin(pix)
    pixels = np.concatenate(
        [np.concatenate([pix_cos, pix_sin], 1), np.concatenate([-pix_sin, pix_cos], 1)], 0
    )
    gap = np.arange(COLS)[None, :] - (COLS // SAMPLES) * np.arange(SAMPLES)[:, None]
    waves = np.arange(1, SAMPLES // 2)
    base = 2.0 * math.pi / COLS
    line = (1.0 + 2.0 * np.cos(base * np.outer(np.arange(COLS), waves)).sum(1)) / SAMPLES
    spread = line[gap % COLS]
    return {
        "rows": split_table(rows),
        "rows_back": split_table(2.0 * rows),
        "band": split_table(band),
        "band_back": split_table(band.T),
        "edge": split_table(edge),
        "edge_back": edge[:8].astype(np.float32),
        "unfold": unfold.astype(ml_dtypes.bfloat16),
        "fold": unfold.T.astype(ml_dtypes.bfloat16),
        "flip": flip.astype(ml_dtypes.bfloat16),
        "flip_back": flip.T.astype(ml_dtypes.bfloat16),
        "out": split_table(out_rows),
        "out_back": split_table(out_rows.transpose(0, 2, 1)),
        "pixels": split_table(pixels),
        "pixels_back": split_table(pixels.T),
        "spread": split_table(spread),
        "spread_back": split_table(spread.T),
    }


def split(value):
    high = value.astype(BF16)
    low = (value - high.astype(F32)).astype(BF16)
    return high, low


def dot(former, latter):
    return lax.dot_general(
        former, latter, (((1,), (0,)), ((), ())), preferred_element_type=F32
    )


def dot_last(former, latter):
    return lax.dot_general(
        former, latter, (((1,), (1,)), ((), ())), preferred_element_type=F32
    )


def dot3(former, latter, dot=dot):
    return (
        dot(former[0], latter[0]) + dot(former[0], latter[1]) + dot(former[1], latter[0])
    )


def pair(ref):
    return ref[0], ref[1]


def moved(flip, value):
    high, rest = value.astype(BF16), value
    total = dot(flip, high)
    for _ in range(2):
        rest = rest - high.astype(F32)
        high = rest.astype(BF16)
        total = total + dot(flip, high)
    return total


def moved_right(value, flip):
    high, rest = value.astype(BF16), value
    total = dot(high, flip)
    for _ in range(2):
        rest = rest - high.astype(F32)
        high = rest.astype(BF16)
        total = total + dot(high, flip)
    return total


def window_kernel(above_ref, mask_ref, below_ref, rows_ref, out_ref):
    tile = lax.axis_index("tile")
    last = lax.axis_size("tile") - 1
    above = jnp.where(tile > 0, above_ref[:, TILE - HALO :], 0.0)
    below = jnp.where(tile < last, below_ref[:, :HALO], 0.0)
    window = jnp.concatenate([above, mask_ref[...], below], 1)
    done = dot3(pair(rows_ref), split(window), dot_last)
    out_ref[...] = jnp.concatenate([done[:HALF], done[HALF:]], 1)


def padded(row):
    return jnp.concatenate([row, jnp.zeros((1, FREQS - HALF), F32)], 1)


def with_edges(value, edges, weights=()):
    row = lax.broadcasted_iota(jnp.int32, value.shape, 0)
    for slot, edge in enumerate(edges):
        value = jnp.where(row == EDGE_ROW + slot, padded(edge), value)
    for slot, weight in enumerate(weights):
        value = jnp.where(row == WEIGHT_ROW + slot, weight, value)
    return value


def edge_columns(value):
    columns = value[HALF - 8 : HALF].T[:HALF]
    first = EDGE_ROW - (HALF - 8)
    return jnp.concatenate([columns[:, first : first + 1], columns[:, first + 1 : first + 2]], 0)


def band_kernel(
    weight_ref, r0, r1, r2, r3, band_ref, edge_ref, out_ref, order_ref
):
    kern = lax.axis_index("kern")
    at_y, at_z = kern // 4, kern % 4
    for step, ref in enumerate((r0, r1, r2, r3)):
        order_ref[pl.ds((at_z + step) % 4, 1)] = ref[...][None]
    blocks = [order_ref[slot] for slot in range(4)]
    cos = jnp.concatenate([block[:, :SHARD] for block in blocks], 1)
    sin = jnp.concatenate([block[:, SHARD:] for block in blocks], 1)
    rows = split(jnp.concatenate([cos, sin], 0))
    start = pl.multiple_of(at_y * WIDE, WIDE)
    band = tuple(band_ref[i, pl.ds(start, WIDE), :] for i in range(2))
    edge = tuple(edge_ref[i, :, pl.ds(start, WIDE)] for i in range(2))
    done = dot3(rows, band)
    edges = dot3(edge, rows, dot_last)[:1]
    out_ref[...] = with_edges(
        done, (edges[:, :HALF], edges[:, HALF:]), (weight_ref[0], weight_ref[1])
    )


def aerial_kernel(
    p0, p1, p2, p3, h0, h1, h2, h3, unfold_ref, flip_ref, out_rows_ref, pixels_ref,
    field_ref, image_ref,
):
    at_y = lax.axis_index("kern") // 4
    total = (p0[...] + p1[...]) + (p2[...] + p3[...])
    done = moved_right(total, unfold_ref[...])
    lane = lax.broadcasted_iota(jnp.int32, done.shape, 1)
    done = jnp.where(lane == FREQS, edge_columns(total), done)
    cos_cos, cos_sin = done[:HALF, :FREQS], done[:HALF, FREQS:]
    sin_cos, sin_sin = done[HALF:, :FREQS], done[HALF:, FREQS:]
    plus = jnp.concatenate([cos_cos - sin_sin, -(cos_sin + sin_cos)], 1)
    minus = jnp.concatenate([cos_cos + sin_sin, sin_cos - cos_sin], 1)
    spectrum = jnp.concatenate([moved(flip_ref[...], minus), plus[: FREQS // 2]], 0)
    spec_re, spec_im = spectrum[:, :FREQS], spectrum[:, FREQS:]
    out_rows = (
        out_rows_ref[0, pl.ds(at_y, 1)][0],
        out_rows_ref[1, pl.ds(at_y, 1)][0],
    )
    mids = []
    weights = []
    for part_ref, kernel_ref in zip((p0, p1, p2, p3), (h0, h1, h2, h3)):
        for slot in range(2):
            kern_re, kern_im = kernel_ref[slot, 0], kernel_ref[slot, 1]
            row = WEIGHT_ROW + slot
            weights.append(part_ref[row : row + 1, :1])
            band = jnp.concatenate(
                [
                    kern_re * spec_re - kern_im * spec_im,
                    kern_re * spec_im + kern_im * spec_re,
                ],
                1,
            )
            quads = dot3(out_rows, split(band))
            upper, lower = quads[:QUARTER], quads[QUARTER:]
            mids.append(
                jnp.concatenate(
                    [
                        upper[:, :FREQS] - lower[:, FREQS:],
                        upper[:, FREQS:] + lower[:, :FREQS],
                    ],
                    1,
                )
            )
    field = dot3(split(jnp.concatenate(mids, 0)), pair(pixels_ref))
    image = None
    for slot in range(COUNT):
        part = field[slot * QUARTER : (slot + 1) * QUARTER]
        heavy = part * weights[slot]
        field_ref[slot * QUARTER : (slot + 1) * QUARTER, :] = heavy
        part = part * heavy
        part = part[:, :SAMPLES] + part[:, SAMPLES:]
        image = part if image is None else image + part
    image_ref[...] = image


def slope_kernel(
    i0, i1, i2, i3, goal_ref, field_ref, h0, h1, h2, h3,
    spread_ref, spread_back_ref, pixels_back_ref, out_back_ref, flip_back_ref,
    fold_ref, m0, m1, m2, m3, resist_ref,
):
    kern = lax.axis_index("kern")
    at_y, at_z = kern // 4, kern % 4
    image = (i0[...] + i1[...]) + (i2[...] + i3[...])
    image = dot3(split(image), pair(spread_ref))
    resist = 1.0 / (1.0 + jnp.exp(-STEEPNESS * (image - THRESHOLD)))
    goal = goal_ref[...].astype(F32)
    slope = 2.0 * STEEPNESS * (resist - goal) * resist * (1.0 - resist)
    slope = slope.astype(BF16)
    slope = dot(slope, spread_back_ref[0]) + dot(slope, spread_back_ref[1])
    slope = jnp.concatenate([slope, slope], 1)
    weighted = jnp.concatenate(
        [slope * field_ref[slot * QUARTER : (slot + 1) * QUARTER, :] for slot in range(COUNT)], 0
    )
    freqs = dot3(split(weighted), pair(pixels_back_ref))
    out_back = (
        out_back_ref[0, pl.ds(at_y, 1)][0],
        out_back_ref[1, pl.ds(at_y, 1)][0],
    )
    grad_re = grad_im = None
    for slot in range(COUNT):
        kernel_ref = (h0, h1, h2, h3)[slot // 2]
        kern_re, kern_im = kernel_ref[slot % 2, 0], kernel_ref[slot % 2, 1]
        part = freqs[slot * QUARTER : (slot + 1) * QUARTER]
        block = jnp.concatenate(
            [part, jnp.concatenate([part[:, FREQS:], -part[:, :FREQS]], 1)], 0
        )
        adjoint = dot3(out_back, split(block))
        adj_re, adj_im = adjoint[:, :FREQS], adjoint[:, FREQS:]
        term_re = kern_re * adj_re + kern_im * adj_im
        term_im = kern_re * adj_im - kern_im * adj_re
        grad_re = term_re if grad_re is None else grad_re + term_re
        grad_im = term_im if grad_im is None else grad_im + term_im
    grad = jnp.concatenate([grad_re, grad_im], 1)
    plus = jnp.concatenate(
        [grad[FREQS // 2 :], jnp.zeros((HALF - FREQS // 2, 2 * FREQS), F32)], 0
    )
    minus = moved(flip_back_ref[...], grad[: FREQS // 2])
    both, less = plus + minus, minus - plus
    done = jnp.concatenate(
        [
            jnp.concatenate([both[:, :FREQS], -both[:, FREQS:]], 1),
            jnp.concatenate([less[:, FREQS:], less[:, :FREQS]], 1),
        ],
        0,
    )
    first = done[:, FREQS : FREQS + 8].T[:1]
    done = moved_right(done, fold_ref[...])
    done = with_edges(done, (first[:, :HALF], first[:, HALF:]))
    resist_ref[...] = resist
    for step, message in enumerate((m0, m1, m2, m3)):
        message[: 2 * HALF, :] = done
        block = 4 * ((at_y + step) % 4) + at_z
        start = pl.multiple_of((block // 2) * 2 * SHARD, 2 * SHARD)
        wide = resist_ref[:, pl.ds(start, 2 * SHARD)].T
        piece = jnp.where(block % 2 == 0, wide[:SHARD], wide[SHARD:])
        message[2 * HALF :, :] = jnp.concatenate([piece[:EXTRA], piece[EXTRA:]], 1)


def columns_kernel(
    m0, m1, m2, m3, band_back_ref, edge_ref, g0, g1, g2, g3, resist_ref, order_ref
):
    kern = lax.axis_index("kern")
    at_y, at_z = kern // 4, kern % 4
    rows = slice(0, 2 * HALF)
    total = (m0[rows] + m1[rows]) + (m2[rows] + m3[rows])
    start = pl.multiple_of(at_y * WIDE, WIDE)
    band = tuple(band_back_ref[i, :, pl.ds(start, WIDE)] for i in range(2))
    done = dot3(split(total), band)
    done = done + edge_columns(total) * edge_ref[:1, pl.ds(start, WIDE)]
    for slot in range(4):
        cols = slice(slot * SHARD, (slot + 1) * SHARD)
        order_ref[slot] = jnp.concatenate([done[:HALF, cols], done[HALF:, cols]], 1)
    for step, out in enumerate((g0, g1, g2, g3)):
        out[...] = order_ref[pl.ds((at_z + step) % 4, 1)][0]
    pieces = []
    for message in (m0, m1, m2, m3):
        piece = message[2 * HALF :, :]
        pieces.append(jnp.concatenate([piece[:, :SHARD], piece[:, SHARD:]], 0))
    spots = []
    for slot in range(4):
        spot = pieces[0]
        for step in (1, 2, 3):
            spot = jnp.where((at_y - step + 4) % 4 == slot, pieces[step], spot)
        spots.append(spot)
    resist_ref[...] = jnp.concatenate(spots, 1)


def stack(value):
    value = value.T
    return split(value[:SHARD]), split(value[SHARD:])


def final_kernel(above_ref, own_ref, below_ref, rows_ref, out_ref):
    tile = lax.axis_index("tile")
    last = lax.axis_size("tile") - 1
    above = stack(jnp.where(tile > 0, above_ref[...], 0.0))
    below = stack(jnp.where(tile < last, below_ref[...], 0.0))
    own = stack(own_ref[...])

    def rows(value, first, count):
        total = None
        for half in range(2):
            part = dot3(
                value[half],
                tuple(
                    rows_ref[i, half * HALF : (half + 1) * HALF, first : first + count]
                    for i in range(2)
                ),
            )
            total = part if total is None else total + part
        return total

    out_ref[:, :HALO] = rows(own, HALO, HALO) + rows(above, WINDOW - HALO, HALO)
    out_ref[:, HALO:] = rows(own, 2 * HALO, HALO) + rows(below, 0, HALO)


def call(kernel, shapes, *operands, flops=10**7, smem=(), scratch=()):
    many = isinstance(shapes, list)
    spec = lambda i: pl.BlockSpec(
        memory_space=pltpu.SMEM if i in smem else pltpu.VMEM
    )
    out = [jax.ShapeDtypeStruct(shape, F32) for shape in (shapes if many else [shapes])]
    return pl.pallas_call(
        kernel,
        scratch_shapes=list(scratch),
        out_shape=out if many else out[0],
        in_specs=[spec(i) for i in range(len(operands))],
        out_specs=[pl.BlockSpec(memory_space=pltpu.VMEM)] * len(out)
        if many
        else pl.BlockSpec(memory_space=pltpu.VMEM),
        compiler_params=pltpu.CompilerParams(vmem_limit_bytes=32 * 2**20),
        cost_estimate=pl.CostEstimate(flops=flops, bytes_accessed=10**6, transcendentals=0),
        name=kernel.__name__,
    )(*operands)


def shift_y(value, step):
    route = [(4 * y + z, 4 * ((y + step) % 4) + z) for y in range(4) for z in range(4)]
    return lax.ppermute(value, "kern", route)


def shift_z(value, step):
    route = [(4 * y + z, 4 * y + (z + step) % 4) for y in range(4) for z in range(4)]
    return lax.ppermute(value, "kern", route)


def shift_tile(value, step):
    peers = lax.axis_size("tile")
    return lax.ppermute(value, "tile", [(i, (i + step) % peers) for i in range(peers)])


def per_device(mask_field, target, kernel_spectra, kernel_weight):
    table = {name: jnp.asarray(value) for name, value in tables().items()}
    at_y = lax.axis_index("kern") // 4
    order = [pltpu.VMEM((4, HALF, 2 * SHARD), F32)]
    mask_field = mask_field.T
    above = shift_tile(mask_field, 1)
    below = shift_tile(mask_field, -1)
    kernels = [kernel_spectra] + [shift_y(kernel_spectra, step) for step in (1, 2, 3)]

    rows = call(
        window_kernel, (HALF, 2 * SHARD), above, mask_field, below, table["rows"]
    )
    rows = [rows] + [shift_z(rows, -step) for step in (1, 2, 3)]
    *rows, h1, h2, h3 = lax.optimization_barrier((*rows, *kernels[1:]))
    kernels = [kernel_spectra, h1, h2, h3]
    part = call(
        band_kernel, (2 * HALF, FREQS), kernel_weight, *rows, table["band"],
        table["edge"], smem=(0,), scratch=order,
    )
    parts = [part] + [shift_y(part, step) for step in (1, 2, 3)]
    field, image = call(
        aerial_kernel,
        [(COUNT * QUARTER, 2 * SAMPLES), (QUARTER, SAMPLES)],
        *parts, *kernels, table["unfold"], table["flip"], table["out"],
        table["pixels"], flops=6 * 10**8,
    )
    images = [image] + [shift_z(image, step) for step in (1, 2, 3)]
    goal = lax.dynamic_slice_in_dim(target, at_y * QUARTER, QUARTER, 0)
    *messages, _ = call(
        slope_kernel,
        [(2 * HALF + EXTRA, FREQS)] * 4 + [(QUARTER, COLS)],
        *images, goal, field, *kernels, table["spread"], table["spread_back"],
        table["pixels_back"], table["out_back"], table["flip_back"], table["fold"],
        flops=6 * 10**8,
    )
    messages = [messages[0]] + [shift_y(messages[step], step) for step in (1, 2, 3)]
    *grads, resist = call(
        columns_kernel,
        [(HALF, 2 * SHARD)] * 4 + [(SHARD, TILE)],
        *messages, table["band_back"], table["edge_back"], scratch=order,
    )
    grad = grads[0]
    for step in (1, 2, 3):
        grad = grad + shift_z(grads[step], step)
    mask_grad = call(
        final_kernel, (SHARD, TILE), shift_tile(grad, 1), grad, shift_tile(grad, -1),
        table["rows_back"],
    )
    return (resist.T, mask_grad.T)


def solution(mesh):
    in_specs = (P("tile", "kern"), P("tile", None), P("kern", None, None, None), P("kern"))
    out_specs = (P("tile", "kern"), P("tile", "kern"))
    return jax.shard_map(
        per_device, mesh=mesh, in_specs=in_specs, out_specs=out_specs, check_vma=False
    )
```

```python
import math

import jax
import jax.numpy as jnp
import ml_dtypes
import numpy as np
from jax import lax
from jax.experimental import pallas as pl
from jax.experimental.pallas import tpu as pltpu
from jax.sharding import PartitionSpec as P

COLS = 1024
HALO = 128
FREQS = 128
TILE = 256
WINDOW = 512
SHARD = 64
SAMPLES = 256
QUARTER = 64
COUNT = 8
HALF = 72
EDGE_ROW = 65
WEIGHT_ROW = 67
EXTRA = 32
WIDE = 4 * SHARD
STEEPNESS = 4.0
THRESHOLD = 1.0
F32 = jnp.float32
BF16 = jnp.bfloat16


def angles(places, frequencies, length):
    return (np.outer(places, frequencies) % length) * (2.0 * math.pi / length)


def split_table(value):
    value = value.astype(np.float32)
    high = value.astype(ml_dtypes.bfloat16)
    low = (value - high.astype(np.float32)).astype(ml_dtypes.bfloat16)
    return np.stack([high, low])


def tables():
    freq = np.arange(FREQS) - FREQS // 2
    scale = 1.0 / math.sqrt(WINDOW * COLS)
    win = angles(np.arange(FREQS // 2 + 1), HALO + np.arange(TILE), WINDOW)
    rows = np.zeros((2, HALF, TILE))
    rows[0, : FREQS // 2 + 1] = np.cos(win) * scale
    rows[1, : FREQS // 2 + 1] = np.sin(win) * scale
    rows = rows.reshape(2 * HALF, TILE)
    col = angles(np.arange(COLS), freq, COLS)
    keep = FREQS // 2
    band = np.concatenate([np.cos(col[:, keep:]), np.sin(col[:, keep:])], 1)
    band[:, keep] = np.cos(col[:, 0])
    edge = np.sin(col[:, 0])
    wide = np.zeros((COLS // SHARD, SHARD, 2 * FREQS))
    wide[:, :, :FREQS] = band.reshape(COLS // SHARD, SHARD, FREQS)
    wide[:, :, FREQS] = edge.reshape(COLS // SHARD, SHARD)
    unfold = np.zeros((FREQS, 2 * FREQS))
    for place, value in enumerate(freq):
        size = abs(value)
        unfold[size, place] = 1.0
        if 0 < size < keep:
            unfold[keep + size, FREQS + place] = np.sign(value)
    flip = np.zeros((FREQS // 2, HALF))
    flip[np.arange(FREQS // 2), FREQS // 2 - np.arange(FREQS // 2)] = 1.0
    out = angles(HALO + np.arange(TILE), freq, WINDOW).reshape(4, QUARTER, FREQS)
    out_rows = np.concatenate([np.cos(out), np.sin(out)], 1) / FREQS
    pix = angles(freq, np.arange(SAMPLES), SAMPLES)
    pix_cos, pix_sin = np.cos(pix), np.sin(pix)
    pixels = np.concatenate(
        [np.concatenate([pix_cos, pix_sin], 1), np.concatenate([-pix_sin, pix_cos], 1)], 0
    )
    gap = np.arange(COLS)[None, :] - (COLS // SAMPLES) * np.arange(SAMPLES)[:, None]
    waves = np.arange(1, SAMPLES // 2)
    base = 2.0 * math.pi / COLS
    line = (1.0 + 2.0 * np.cos(base * np.outer(np.arange(COLS), waves)).sum(1)) / SAMPLES
    spread = line[gap % COLS]
    return {
        "rows": split_table(rows),
        "band": split_table(wide),
        "band_back": split_table(band.T),
        "edge_back": np.tile(edge, (8, 1)).astype(np.float32),
        "unfold": unfold.astype(ml_dtypes.bfloat16),
        "fold": unfold.T.astype(ml_dtypes.bfloat16),
        "flip": flip.astype(ml_dtypes.bfloat16),
        "flip_back": flip.T.astype(ml_dtypes.bfloat16),
        "out": split_table(out_rows),
        "out_back": split_table(out_rows.transpose(0, 2, 1)),
        "pixels": split_table(pixels),
        "pixels_back": split_table(pixels.T),
        "spread": split_table(spread),
        "spread_back": split_table(spread.T),
    }


def split(value):
    high = value.astype(BF16)
    low = (value - high.astype(F32)).astype(BF16)
    return high, low


def dot(former, latter):
    return lax.dot_general(
        former, latter, (((1,), (0,)), ((), ())), preferred_element_type=F32
    )


def dot_last(former, latter):
    return lax.dot_general(
        former, latter, (((1,), (1,)), ((), ())), preferred_element_type=F32
    )


def dot3(former, latter, dot=dot):
    return (
        dot(former[0], latter[0]) + dot(former[0], latter[1]) + dot(former[1], latter[0])
    )


def pair(ref):
    return ref[0], ref[1]


def moved(flip, value):
    high, rest = value.astype(BF16), value
    total = dot(flip, high)
    for _ in range(2):
        rest = rest - high.astype(F32)
        high = rest.astype(BF16)
        total = total + dot(flip, high)
    return total


def moved_right(value, flip):
    high, rest = value.astype(BF16), value
    total = dot(high, flip)
    for _ in range(2):
        rest = rest - high.astype(F32)
        high = rest.astype(BF16)
        total = total + dot(high, flip)
    return total


def pair_up(value):
    return jnp.concatenate([value[:HALF], value[HALF:]], 1)


def alternate(shape):
    return 1.0 - 2.0 * (lax.broadcasted_iota(jnp.int32, shape, 0) % 2).astype(F32)


def weight_kernel(weight_ref, out_ref):
    row = lax.broadcasted_iota(jnp.int32, out_ref.shape, 0)
    out_ref[...] = jnp.where(row == WEIGHT_ROW - HALF + 8, weight_ref[0], weight_ref[1])


def window_kernel(above_ref, below_ref, mask_ref, rows_ref, heavy_ref, out_ref):
    tile = lax.axis_index("tile")
    last = lax.axis_size("tile") - 1
    above = jnp.where(tile > 0, above_ref[:, TILE - HALO :], 0.0)
    below = jnp.where(tile < last, below_ref[:, :HALO], 0.0)
    sides = jnp.concatenate([below, above], 1)
    both = split(jnp.concatenate([mask_ref[...], sides], 0))
    done = dot3(pair(rows_ref), both, dot_last)
    own, halo = done[:, :SHARD], done[:, SHARD:]
    done = pair_up(own) + alternate((HALF, 2 * SHARD)) * pair_up(halo)
    row = lax.broadcasted_iota(jnp.int32, (8, 2 * SHARD), 0) + HALF - 8
    out_ref[: HALF - 8] = done[: HALF - 8]
    out_ref[HALF - 8 :] = jnp.where(row < WEIGHT_ROW, done[HALF - 8 :], heavy_ref[...])


def padded(row):
    return jnp.concatenate([row, jnp.zeros((1, FREQS - HALF), F32)], 1)


def with_edges(value, edges, weights=None):
    row = lax.broadcasted_iota(jnp.int32, value.shape, 0)
    for slot, edge in enumerate(edges):
        value = jnp.where(row == EDGE_ROW + slot, padded(edge), value)
    if weights is None:
        return value
    heavy = jnp.concatenate([value[: HALF - 8], weights, value[HALF:]], 0)
    return jnp.where((row >= WEIGHT_ROW) & (row < HALF), heavy, value)


def edge_columns(value):
    columns = value[HALF - 8 : HALF].T[:HALF]
    first = EDGE_ROW - (HALF - 8)
    return jnp.concatenate([columns[:, first : first + 1], columns[:, first + 1 : first + 2]], 0)


def band_kernel(r0, r1, r2, r3, band_ref, out_ref):
    kern = lax.axis_index("kern")
    at_y, at_z = kern // 4, kern % 4
    blocks = [ref[...] for ref in (r0, r1, r2, r3)]
    cos = jnp.concatenate([block[:, :SHARD] for block in blocks], 1)
    sin = jnp.concatenate([block[:, SHARD:] for block in blocks], 1)
    places = [4 * at_y + (at_z + step) % 4 for step in range(4)]
    band = tuple(
        jnp.concatenate([band_ref[i, pl.ds(place, 1)][0] for place in places], 0)
        for i in range(2)
    )
    done = dot3(split(jnp.concatenate([cos, sin], 0)), band)
    edges = [done[half : half + HALF, FREQS:].T[:1] for half in (0, HALF)]
    out_ref[...] = with_edges(done[:, :FREQS], edges, r0[HALF - 8 :])


def aerial_kernel(
    p0, p1, p2, p3, h0, h1, h2, h3, unfold_ref, flip_ref, out_rows_ref, pixels_ref,
    field_ref, image_ref,
):
    at_y = lax.axis_index("kern") // 4
    total = (p0[...] + p1[...]) + (p2[...] + p3[...])
    done = moved_right(total, unfold_ref[...])
    lane = lax.broadcasted_iota(jnp.int32, done.shape, 1)
    done = jnp.where(lane == FREQS, edge_columns(total), done)
    cos_cos, cos_sin = done[:HALF, :FREQS], done[:HALF, FREQS:]
    sin_cos, sin_sin = done[HALF:, :FREQS], done[HALF:, FREQS:]
    plus = jnp.concatenate([cos_cos - sin_sin, -(cos_sin + sin_cos)], 1)
    minus = jnp.concatenate([cos_cos + sin_sin, sin_cos - cos_sin], 1)
    spectrum = jnp.concatenate([moved(flip_ref[...], minus), plus[: FREQS // 2]], 0)
    spec_re, spec_im = spectrum[:, :FREQS], spectrum[:, FREQS:]
    out_rows = (
        out_rows_ref[0, pl.ds(at_y, 1)][0],
        out_rows_ref[1, pl.ds(at_y, 1)][0],
    )
    mids = []
    weights = []
    for part_ref, kernel_ref in zip((p0, p1, p2, p3), (h0, h1, h2, h3)):
        for slot in range(2):
            kern_re, kern_im = kernel_ref[slot, 0], kernel_ref[slot, 1]
            row = WEIGHT_ROW + slot
            weights.append(part_ref[row : row + 1, :1])
            band = jnp.concatenate(
                [
                    kern_re * spec_re - kern_im * spec_im,
                    kern_re * spec_im + kern_im * spec_re,
                ],
                1,
            )
            quads = dot3(out_rows, split(band))
            upper, lower = quads[:QUARTER], quads[QUARTER:]
            mids.append(
                jnp.concatenate(
                    [
                        upper[:, :FREQS] - lower[:, FREQS:],
                        upper[:, FREQS:] + lower[:, :FREQS],
                    ],
                    1,
                )
            )
    field = dot3(split(jnp.concatenate(mids, 0)), pair(pixels_ref))
    image = None
    for slot in range(COUNT):
        part = field[slot * QUARTER : (slot + 1) * QUARTER]
        heavy = part * weights[slot]
        field_ref[slot * QUARTER : (slot + 1) * QUARTER, :] = heavy
        part = part * heavy
        part = part[:, :SAMPLES] + part[:, SAMPLES:]
        image = part if image is None else image + part
    image_ref[...] = image


def slope_kernel(
    i0, i1, i2, i3, goal_ref, field_ref, h0, h1, h2, h3,
    spread_ref, spread_back_ref, pixels_back_ref, out_back_ref, flip_back_ref,
    fold_ref, m0, m1, m2, m3, resist_ref,
):
    kern = lax.axis_index("kern")
    at_y, at_z = kern // 4, kern % 4
    image = (i0[...] + i1[...]) + (i2[...] + i3[...])
    image = dot3(split(image), pair(spread_ref))
    resist = 1.0 / (1.0 + jnp.exp(-STEEPNESS * (image - THRESHOLD)))
    goal = goal_ref[...].astype(F32)
    slope = 2.0 * STEEPNESS * (resist - goal) * resist * (1.0 - resist)
    slope = slope.astype(BF16)
    slope = dot(slope, spread_back_ref[0]) + dot(slope, spread_back_ref[1])
    slope = jnp.concatenate([slope, slope], 1)
    weighted = jnp.concatenate(
        [slope * field_ref[slot * QUARTER : (slot + 1) * QUARTER, :] for slot in range(COUNT)], 0
    )
    freqs = dot3(split(weighted), pair(pixels_back_ref))
    out_back = (
        out_back_ref[0, pl.ds(at_y, 1)][0],
        out_back_ref[1, pl.ds(at_y, 1)][0],
    )
    grad_re = grad_im = None
    for slot in range(COUNT):
        kernel_ref = (h0, h1, h2, h3)[slot // 2]
        kern_re, kern_im = kernel_ref[slot % 2, 0], kernel_ref[slot % 2, 1]
        part = freqs[slot * QUARTER : (slot + 1) * QUARTER]
        block = jnp.concatenate(
            [part, jnp.concatenate([part[:, FREQS:], -part[:, :FREQS]], 1)], 0
        )
        adjoint = dot3(out_back, split(block))
        adj_re, adj_im = adjoint[:, :FREQS], adjoint[:, FREQS:]
        term_re = kern_re * adj_re + kern_im * adj_im
        term_im = kern_re * adj_im - kern_im * adj_re
        grad_re = term_re if grad_re is None else grad_re + term_re
        grad_im = term_im if grad_im is None else grad_im + term_im
    grad = jnp.concatenate([grad_re, grad_im], 1)
    plus = jnp.concatenate(
        [grad[FREQS // 2 :], jnp.zeros((HALF - FREQS // 2, 2 * FREQS), F32)], 0
    )
    minus = moved(flip_back_ref[...], grad[: FREQS // 2])
    both, less = plus + minus, minus - plus
    done = jnp.concatenate(
        [
            jnp.concatenate([both[:, :FREQS], -both[:, FREQS:]], 1),
            jnp.concatenate([less[:, FREQS:], less[:, :FREQS]], 1),
        ],
        0,
    )
    first = done[:, FREQS : FREQS + 8].T[:1]
    done = moved_right(done, fold_ref[...])
    done = with_edges(done, (first[:, :HALF], first[:, HALF:]))
    resist_ref[...] = resist
    for step, message in enumerate((m0, m1, m2, m3)):
        message[: 2 * HALF, :] = done
        block = 4 * ((at_y + step) % 4) + at_z
        start = pl.multiple_of((block // 2) * 2 * SHARD, 2 * SHARD)
        wide = resist_ref[:, pl.ds(start, 2 * SHARD)].T
        piece = jnp.where(block % 2 == 0, wide[:SHARD], wide[SHARD:])
        message[2 * HALF :, :] = jnp.concatenate([piece[:EXTRA], piece[EXTRA:]], 1)


def columns_kernel(
    m0, m1, m2, m3, band_back_ref, edge_ref, g0, g1, g2, g3, order_ref
):
    kern = lax.axis_index("kern")
    at_y, at_z = kern // 4, kern % 4
    rows = slice(0, 2 * HALF)
    total = (m0[rows] + m1[rows]) + (m2[rows] + m3[rows])
    start = pl.multiple_of(at_y * WIDE, WIDE)
    band = tuple(band_back_ref[i, :, pl.ds(start, WIDE)] for i in range(2))
    done = dot3(split(total), band)
    done = done + edge_columns(total) * edge_ref[:1, pl.ds(start, WIDE)]
    for slot in range(4):
        cols = slice(slot * SHARD, (slot + 1) * SHARD)
        order_ref[slot] = jnp.concatenate([done[:HALF, cols], done[HALF:, cols]], 1)
    for step, out in enumerate((g0, g1, g2, g3)):
        out[...] = order_ref[pl.ds((at_z + step) % 4, 1)][0]


def resist_kernel(m0, m1, m2, m3, resist_ref):
    at_y = lax.axis_index("kern") // 4
    pieces = []
    for message in (m0, m1, m2, m3):
        piece = message[2 * HALF :, :]
        pieces.append(jnp.concatenate([piece[:, :SHARD], piece[:, SHARD:]], 0))
    spots = []
    for slot in range(4):
        spot = pieces[0]
        for step in (1, 2, 3):
            spot = jnp.where((at_y - step + 4) % 4 == slot, pieces[step], spot)
        spots.append(spot)
    resist_ref[...] = jnp.concatenate(spots, 1)


def final_kernel(above_ref, own_ref, below_ref, rows_ref, out_ref):
    tile = lax.axis_index("tile")
    last = lax.axis_size("tile") - 1
    own = own_ref[...]
    sign = 2.0 * alternate(own.shape)
    own = 2.0 * own
    sides = (
        own + jnp.where(tile > 0, above_ref[...], 0.0) * sign,
        own + jnp.where(tile < last, below_ref[...], 0.0) * sign,
    )
    for slot, side in enumerate(sides):
        side = split(side.T)
        cols = slice(slot * HALO, (slot + 1) * HALO)
        total = None
        for half in range(2):
            part = dot3(
                (side[0][half * SHARD : (half + 1) * SHARD], side[1][half * SHARD : (half + 1) * SHARD]),
                tuple(rows_ref[i, half * HALF : (half + 1) * HALF, cols] for i in range(2)),
            )
            total = part if total is None else total + part
        out_ref[:, cols] = total


def call(kernel, shapes, *operands, flops=4 * 10**9, smem=(), hbm=(), scratch=()):
    many = isinstance(shapes, list)
    space = lambda i: pltpu.SMEM if i in smem else pltpu.HBM if i in hbm else pltpu.VMEM
    spec = lambda i: pl.BlockSpec(memory_space=space(i))
    out = [jax.ShapeDtypeStruct(shape, F32) for shape in (shapes if many else [shapes])]
    return pl.pallas_call(
        kernel,
        scratch_shapes=list(scratch),
        out_shape=out if many else out[0],
        in_specs=[spec(i) for i in range(len(operands))],
        out_specs=[pl.BlockSpec(memory_space=pltpu.VMEM)] * len(out)
        if many
        else pl.BlockSpec(memory_space=pltpu.VMEM),
        compiler_params=pltpu.CompilerParams(vmem_limit_bytes=32 * 2**20),
        cost_estimate=pl.CostEstimate(flops=flops, bytes_accessed=10**6, transcendentals=0),
        name=kernel.__name__,
    )(*operands)


def shift_y(value, step):
    route = [(4 * y + z, 4 * ((y + step) % 4) + z) for y in range(4) for z in range(4)]
    return lax.ppermute(value, "kern", route)


def shift_z(value, step):
    route = [(4 * y + z, 4 * y + (z + step) % 4) for y in range(4) for z in range(4)]
    return lax.ppermute(value, "kern", route)


def shift_tile(value, step):
    peers = lax.axis_size("tile")
    return lax.ppermute(value, "tile", [(i, (i + step) % peers) for i in range(peers)])


def per_device(mask_field, target, kernel_spectra, kernel_weight):
    table = {name: jnp.asarray(value) for name, value in tables().items()}
    at_y = lax.axis_index("kern") // 4
    order = [pltpu.VMEM((4, HALF, 2 * SHARD), F32)]
    mask_field = mask_field.T
    above = shift_tile(mask_field, 1)
    below = shift_tile(mask_field, -1)
    heavy = call(weight_kernel, (8, 2 * SHARD), kernel_weight, smem=(0,))
    kernel_spectra, heavy = lax.optimization_barrier((kernel_spectra, heavy))
    kernels = [kernel_spectra] + [shift_y(kernel_spectra, step) for step in (1, 2, 3)]

    rows = call(
        window_kernel, (HALF, 2 * SHARD), above, below, mask_field, table["rows"], heavy
    )
    rows = [rows] + [shift_z(rows, -step) for step in (1, 2, 3)]
    *rows, h1, h3 = lax.optimization_barrier((*rows, kernels[1], kernels[3]))
    kernels = [kernel_spectra, h1, kernels[2], h3]
    part = call(
        band_kernel, (2 * HALF, FREQS), *rows, table["band"]
    )
    parts = [part] + [shift_y(part, step) for step in (1, 2, 3)]
    field, image = call(
        aerial_kernel,
        [(COUNT * QUARTER, 2 * SAMPLES), (QUARTER, SAMPLES)],
        *parts, *kernels, table["unfold"], table["flip"], table["out"],
        table["pixels"], flops=4 * 10**9,
    )
    images = [image] + [shift_z(image, step) for step in (1, 2, 3)]
    goal = lax.dynamic_slice_in_dim(target, at_y * QUARTER, QUARTER, 0)
    messages = call(
        slope_kernel,
        [(2 * HALF + EXTRA, FREQS)] * 4,
        *images, goal, field, *kernels, table["spread"], table["spread_back"],
        table["pixels_back"], table["out_back"], table["flip_back"], table["fold"],
        scratch=[pltpu.VMEM((QUARTER, COLS), F32)],
    )
    messages = [messages[0]] + [shift_y(messages[step], step) for step in (1, 2, 3)]
    resist = call(resist_kernel, (SHARD, TILE), *messages)
    grads = call(
        columns_kernel,
        [(HALF, 2 * SHARD)] * 4,
        *messages, table["band_back"], table["edge_back"], scratch=order,
    )
    grad = grads[0]
    for step in (1, 2, 3):
        grad = grad + shift_z(grads[step], step)
    mask_grad = call(
        final_kernel, (SHARD, TILE), shift_tile(grad, 1), grad, shift_tile(grad, -1),
        table["rows"],
    )
    return (resist.T, mask_grad.T)


def solution(mesh):
    in_specs = (P("tile", "kern"), P("tile", None), P("kern", None, None, None), P("kern"))
    out_specs = (P("tile", "kern"), P("tile", "kern"))
    return jax.shard_map(
        per_device, mesh=mesh, in_specs=in_specs, out_specs=out_specs, check_vma=False
    )
```

```python
import math

import jax
import jax.numpy as jnp
import ml_dtypes
import numpy as np
from jax import lax
from jax.experimental import pallas as pl
from jax.experimental.pallas import tpu as pltpu
from jax.sharding import PartitionSpec as P

COLS = 1024
HALO = 128
FREQS = 128
TILE = 256
WINDOW = 512
SHARD = 64
SAMPLES = 256
QUARTER = 64
COUNT = 8
HALF = 72
EDGE_ROW = 65
WEIGHT_ROW = 67
EXTRA = 32
WIDE = 4 * SHARD
STEEPNESS = 4.0
THRESHOLD = 1.0
F32 = jnp.float32
BF16 = jnp.bfloat16


def angles(places, frequencies, length):
    return (np.outer(places, frequencies) % length) * (2.0 * math.pi / length)


def split_table(value):
    value = value.astype(np.float32)
    high = value.astype(ml_dtypes.bfloat16)
    low = (value - high.astype(np.float32)).astype(ml_dtypes.bfloat16)
    return np.stack([high, low])


def tables():
    freq = np.arange(FREQS) - FREQS // 2
    scale = 1.0 / math.sqrt(WINDOW * COLS)
    win = angles(np.arange(FREQS // 2 + 1), HALO + np.arange(TILE), WINDOW)
    rows = np.zeros((2, HALF, TILE))
    rows[0, : FREQS // 2 + 1] = np.cos(win) * scale
    rows[1, : FREQS // 2 + 1] = np.sin(win) * scale
    rows = rows.reshape(2 * HALF, TILE)
    col = angles(np.arange(COLS), freq, COLS)
    keep = FREQS // 2
    band = np.concatenate([np.cos(col[:, keep:]), np.sin(col[:, keep:])], 1)
    band[:, keep] = np.cos(col[:, 0])
    edge = np.sin(col[:, 0])
    wide = np.zeros((COLS // SHARD, SHARD, 2 * FREQS))
    wide[:, :, :FREQS] = band.reshape(COLS // SHARD, SHARD, FREQS)
    wide[:, :, FREQS] = edge.reshape(COLS // SHARD, SHARD)
    unfold = np.zeros((FREQS, 2 * FREQS))
    for place, value in enumerate(freq):
        size = abs(value)
        unfold[size, place] = 1.0
        if 0 < size < keep:
            unfold[keep + size, FREQS + place] = np.sign(value)
    flip = np.zeros((FREQS // 2, HALF))
    flip[np.arange(FREQS // 2), FREQS // 2 - np.arange(FREQS // 2)] = 1.0
    out = angles(HALO + np.arange(TILE), freq, WINDOW).reshape(4, QUARTER, FREQS)
    out_rows = np.concatenate([np.cos(out), np.sin(out)], 1) / FREQS
    pix = angles(freq, np.arange(SAMPLES), SAMPLES)
    pix_cos, pix_sin = np.cos(pix), np.sin(pix)
    pixels = np.concatenate(
        [np.concatenate([pix_cos, pix_sin], 1), np.concatenate([-pix_sin, pix_cos], 1)], 0
    )
    gap = np.arange(COLS)[None, :] - (COLS // SAMPLES) * np.arange(SAMPLES)[:, None]
    waves = np.arange(1, SAMPLES // 2)
    base = 2.0 * math.pi / COLS
    line = (1.0 + 2.0 * np.cos(base * np.outer(np.arange(COLS), waves)).sum(1)) / SAMPLES
    spread = line[gap % COLS]
    return {
        "rows": split_table(rows),
        "band": split_table(wide),
        "band_back": split_table(band.T),
        "edge_back": np.tile(edge, (8, 1)).astype(np.float32),
        "unfold": unfold.astype(ml_dtypes.bfloat16),
        "fold": unfold.T.astype(ml_dtypes.bfloat16),
        "flip": flip.astype(ml_dtypes.bfloat16),
        "flip_back": flip.T.astype(ml_dtypes.bfloat16),
        "out": split_table(out_rows),
        "out_back": split_table(out_rows.transpose(0, 2, 1)),
        "pixels": split_table(pixels),
        "pixels_back": split_table(pixels.T),
        "spread": split_table(spread),
        "spread_back": split_table(spread.T),
    }


def split(value):
    high = value.astype(BF16)
    low = (value - high.astype(F32)).astype(BF16)
    return high, low


def dot(former, latter):
    return lax.dot_general(
        former, latter, (((1,), (0,)), ((), ())), preferred_element_type=F32
    )


def dot_last(former, latter):
    return lax.dot_general(
        former, latter, (((1,), (1,)), ((), ())), preferred_element_type=F32
    )


def dot3(former, latter, dot=dot):
    return (
        dot(former[0], latter[0]) + dot(former[0], latter[1]) + dot(former[1], latter[0])
    )


def dot3_deep(former, latter):
    twice = jnp.concatenate([former[0], former[0]], 1)
    return dot(twice, jnp.concatenate(latter, 0)) + dot(former[1], latter[0])


def pair(ref):
    return ref[0], ref[1]


def moved(flip, value):
    high, low = split(value)
    return dot(flip, high) + dot(flip, low)


def moved_right(value, flip):
    high, low = split(value)
    return dot(high, flip) + dot(low, flip)


def pair_up(value):
    return jnp.concatenate([value[:HALF], value[HALF:]], 1)


def alternate(shape):
    return 1.0 - 2.0 * (lax.broadcasted_iota(jnp.int32, shape, 0) % 2).astype(F32)


def weight_kernel(weight_ref, out_ref):
    row = lax.broadcasted_iota(jnp.int32, out_ref.shape, 0)
    out_ref[...] = jnp.where(row == WEIGHT_ROW - HALF + 8, weight_ref[0], weight_ref[1])


def neighbours(outer, inner):
    tile = lax.axis_index("tile")
    last = lax.axis_size("tile") - 1
    outer = jnp.where((tile > 0) & (tile < last), outer, 0.0)
    odd = tile % 2 == 1
    return jnp.where(odd, inner, outer), jnp.where(odd, outer, inner)


def window_kernel(outer_ref, inner_ref, mask_ref, rows_ref, heavy_ref, out_ref):
    above, below = neighbours(outer_ref[...], inner_ref[...])
    above, below = above[:, TILE - HALO :], below[:, :HALO]
    sides = jnp.concatenate([below, above], 1)
    both = split(jnp.concatenate([mask_ref[...], sides], 0))
    done = dot3(pair(rows_ref), both, dot_last)
    own, halo = done[:, :SHARD], done[:, SHARD:]
    done = pair_up(own) + alternate((HALF, 2 * SHARD)) * pair_up(halo)
    row = lax.broadcasted_iota(jnp.int32, (8, 2 * SHARD), 0) + HALF - 8
    out_ref[: HALF - 8] = done[: HALF - 8]
    out_ref[HALF - 8 :] = jnp.where(row < WEIGHT_ROW, done[HALF - 8 :], heavy_ref[...])


def padded(row):
    return jnp.concatenate([row, jnp.zeros((1, FREQS - HALF), F32)], 1)


def with_edges(value, edges, weights=None):
    row = lax.broadcasted_iota(jnp.int32, value.shape, 0)
    for slot, edge in enumerate(edges):
        value = jnp.where(row == EDGE_ROW + slot, padded(edge), value)
    if weights is None:
        return value
    heavy = jnp.concatenate([value[: HALF - 8], weights, value[HALF:]], 0)
    return jnp.where((row >= WEIGHT_ROW) & (row < HALF), heavy, value)


def edge_columns(value):
    columns = value[HALF - 8 : HALF].T[:HALF]
    first = EDGE_ROW - (HALF - 8)
    return jnp.concatenate([columns[:, first : first + 1], columns[:, first + 1 : first + 2]], 0)


def band_kernel(r0, r1, r2, r3, band_ref, out_ref):
    kern = lax.axis_index("kern")
    at_y, at_z = kern // 4, kern % 4
    blocks = [ref[...] for ref in (r0, r1, r2, r3)]
    cos = jnp.concatenate([block[:, :SHARD] for block in blocks], 1)
    sin = jnp.concatenate([block[:, SHARD:] for block in blocks], 1)
    places = [4 * at_y + (at_z ^ step) for step in range(4)]
    band = tuple(
        jnp.concatenate([band_ref[i, pl.ds(place, 1)][0] for place in places], 0)
        for i in range(2)
    )
    done = dot3(split(jnp.concatenate([cos, sin], 0)), band)
    edges = [done[half : half + HALF, FREQS:].T[:1] for half in (0, HALF)]
    out_ref[...] = with_edges(done[:, :FREQS], edges, r0[HALF - 8 :])


def aerial_kernel(
    p0, p1, p2, p3, h0, h1, h2, h3, unfold_ref, flip_ref, out_rows_ref, pixels_ref,
    field_ref, image_ref,
):
    at_y = lax.axis_index("kern") // 4
    total = (p0[...] + p1[...]) + (p2[...] + p3[...])
    done = moved_right(total, unfold_ref[...])
    lane = lax.broadcasted_iota(jnp.int32, done.shape, 1)
    done = jnp.where(lane == FREQS, edge_columns(total), done)
    cos_cos, cos_sin = done[:HALF, :FREQS], done[:HALF, FREQS:]
    sin_cos, sin_sin = done[HALF:, :FREQS], done[HALF:, FREQS:]
    plus = jnp.concatenate([cos_cos - sin_sin, -(cos_sin + sin_cos)], 1)
    minus = jnp.concatenate([cos_cos + sin_sin, sin_cos - cos_sin], 1)
    spectrum = jnp.concatenate([moved(flip_ref[...], minus), plus[: FREQS // 2]], 0)
    spec_re, spec_im = spectrum[:, :FREQS], spectrum[:, FREQS:]
    out_rows = (
        out_rows_ref[0, pl.ds(at_y, 1)][0],
        out_rows_ref[1, pl.ds(at_y, 1)][0],
    )
    mids = []
    weights = []
    for part_ref, kernel_ref in zip((p0, p1, p2, p3), (h0, h1, h2, h3)):
        for slot in range(2):
            kern_re, kern_im = kernel_ref[slot, 0], kernel_ref[slot, 1]
            row = WEIGHT_ROW + slot
            weights.append(part_ref[row : row + 1, :1])
            band = jnp.concatenate(
                [
                    kern_re * spec_re - kern_im * spec_im,
                    kern_re * spec_im + kern_im * spec_re,
                ],
                1,
            )
            quads = dot3_deep(out_rows, split(band))
            upper, lower = quads[:QUARTER], quads[QUARTER:]
            mids.append(
                jnp.concatenate(
                    [
                        upper[:, :FREQS] - lower[:, FREQS:],
                        upper[:, FREQS:] + lower[:, :FREQS],
                    ],
                    1,
                )
            )
    field = dot3(split(jnp.concatenate(mids, 0)), pair(pixels_ref))
    image = None
    for slot in range(COUNT):
        part = field[slot * QUARTER : (slot + 1) * QUARTER]
        heavy = part * weights[slot]
        field_ref[slot * QUARTER : (slot + 1) * QUARTER, :] = heavy
        part = part * heavy
        part = part[:, :SAMPLES] + part[:, SAMPLES:]
        image = part if image is None else image + part
    image_ref[...] = image


def slope_kernel(
    i0, i1, i2, i3, goal_ref, field_ref, h0, h1, h2, h3,
    spread_ref, spread_back_ref, pixels_back_ref, out_back_ref, flip_back_ref,
    fold_ref, m0, m1, m2, m3, resist_ref,
):
    kern = lax.axis_index("kern")
    at_y, at_z = kern // 4, kern % 4
    image = (i0[...] + i1[...]) + (i2[...] + i3[...])
    image = dot3(split(image), pair(spread_ref))
    resist = 1.0 / (1.0 + jnp.exp(-STEEPNESS * (image - THRESHOLD)))
    goal = goal_ref[...].astype(F32)
    slope = 2.0 * STEEPNESS * (resist - goal) * resist * (1.0 - resist)
    slope = slope.astype(BF16)
    slope = dot(slope, spread_back_ref[0]) + dot(slope, spread_back_ref[1])
    slope = jnp.concatenate([slope, slope], 1)
    freqs = []
    for first in range(0, COUNT, 2):
        weighted = jnp.concatenate(
            [
                slope * field_ref[slot * QUARTER : (slot + 1) * QUARTER, :]
                for slot in range(first, first + 2)
            ],
            0,
        )
        freqs.append(dot3(split(weighted), pair(pixels_back_ref)))
    freqs = jnp.concatenate(freqs, 0)
    out_back = (
        out_back_ref[0, pl.ds(at_y, 1)][0],
        out_back_ref[1, pl.ds(at_y, 1)][0],
    )
    grad_re = grad_im = None
    for slot in range(COUNT):
        kernel_ref = (h0, h1, h2, h3)[slot // 2]
        kern_re, kern_im = kernel_ref[slot % 2, 0], kernel_ref[slot % 2, 1]
        part = freqs[slot * QUARTER : (slot + 1) * QUARTER]
        block = jnp.concatenate(
            [part, jnp.concatenate([part[:, FREQS:], -part[:, :FREQS]], 1)], 0
        )
        adjoint = dot3_deep(out_back, split(block))
        adj_re, adj_im = adjoint[:, :FREQS], adjoint[:, FREQS:]
        term_re = kern_re * adj_re + kern_im * adj_im
        term_im = kern_re * adj_im - kern_im * adj_re
        grad_re = term_re if grad_re is None else grad_re + term_re
        grad_im = term_im if grad_im is None else grad_im + term_im
    grad = jnp.concatenate([grad_re, grad_im], 1)
    plus = jnp.concatenate(
        [grad[FREQS // 2 :], jnp.zeros((HALF - FREQS // 2, 2 * FREQS), F32)], 0
    )
    minus = moved(flip_back_ref[...], grad[: FREQS // 2])
    both, less = plus + minus, minus - plus
    done = jnp.concatenate(
        [
            jnp.concatenate([both[:, :FREQS], -both[:, FREQS:]], 1),
            jnp.concatenate([less[:, FREQS:], less[:, :FREQS]], 1),
        ],
        0,
    )
    first = done[:, FREQS : FREQS + 8].T[:1]
    done = moved_right(done, fold_ref[...])
    done = with_edges(done, (first[:, :HALF], first[:, HALF:]))
    resist_ref[...] = resist
    for step, message in enumerate((m0, m1, m2, m3)):
        message[: 2 * HALF, :] = done
        block = 4 * (at_y ^ step) + at_z
        start = pl.multiple_of((block // 2) * 2 * SHARD, 2 * SHARD)
        wide = resist_ref[:, pl.ds(start, 2 * SHARD)].T
        piece = jnp.where(block % 2 == 0, wide[:SHARD], wide[SHARD:])
        message[2 * HALF :, :] = jnp.concatenate([piece[:EXTRA], piece[EXTRA:]], 1)


def columns_kernel(
    m0, m1, m2, m3, band_back_ref, edge_ref, g0, g1, g2, g3, order_ref
):
    kern = lax.axis_index("kern")
    at_y, at_z = kern // 4, kern % 4
    rows = slice(0, 2 * HALF)
    total = (m0[rows] + m1[rows]) + (m2[rows] + m3[rows])
    start = pl.multiple_of(at_y * WIDE, WIDE)
    band = tuple(band_back_ref[i, :, pl.ds(start, WIDE)] for i in range(2))
    done = dot3(split(total), band)
    done = done + edge_columns(total) * edge_ref[:1, pl.ds(start, WIDE)]
    for slot in range(4):
        cols = slice(slot * SHARD, (slot + 1) * SHARD)
        order_ref[slot] = jnp.concatenate([done[:HALF, cols], done[HALF:, cols]], 1)
    for step, out in enumerate((g0, g1, g2, g3)):
        out[...] = order_ref[pl.ds(at_z ^ step, 1)][0]


def resist_kernel(m0, m1, m2, m3, resist_ref):
    at_y = lax.axis_index("kern") // 4
    pieces = []
    for message in (m0, m1, m2, m3):
        piece = message[2 * HALF :, :]
        pieces.append(jnp.concatenate([piece[:, :SHARD], piece[:, SHARD:]], 0))
    spots = []
    for slot in range(4):
        spot = pieces[0]
        for step in (1, 2, 3):
            spot = jnp.where((at_y ^ step) == slot, pieces[step], spot)
        spots.append(spot)
    resist_ref[...] = jnp.concatenate(spots, 1)


def final_kernel(inner_ref, outer_ref, own_ref, rows_ref, out_ref):
    above, below = neighbours(outer_ref[...], inner_ref[...])
    own = own_ref[...]
    sign = 2.0 * alternate(own.shape)
    own = 2.0 * own
    sides = (
        own + above * sign,
        own + below * sign,
    )
    for slot, side in enumerate(sides):
        side = split(side.T)
        cols = slice(slot * HALO, (slot + 1) * HALO)
        total = None
        for half in range(2):
            part = dot3(
                (side[0][half * SHARD : (half + 1) * SHARD], side[1][half * SHARD : (half + 1) * SHARD]),
                tuple(rows_ref[i, half * HALF : (half + 1) * HALF, cols] for i in range(2)),
            )
            total = part if total is None else total + part
        out_ref[:, cols] = total


def call(kernel, shapes, *operands, flops=4 * 10**9, smem=(), hbm=(), scratch=()):
    many = isinstance(shapes, list)
    space = lambda i: pltpu.SMEM if i in smem else pltpu.HBM if i in hbm else pltpu.VMEM
    spec = lambda i: pl.BlockSpec(memory_space=space(i))
    out = [jax.ShapeDtypeStruct(shape, F32) for shape in (shapes if many else [shapes])]
    return pl.pallas_call(
        kernel,
        scratch_shapes=list(scratch),
        out_shape=out if many else out[0],
        in_specs=[spec(i) for i in range(len(operands))],
        out_specs=[pl.BlockSpec(memory_space=pltpu.VMEM)] * len(out)
        if many
        else pl.BlockSpec(memory_space=pltpu.VMEM),
        compiler_params=pltpu.CompilerParams(vmem_limit_bytes=32 * 2**20),
        cost_estimate=pl.CostEstimate(flops=flops, bytes_accessed=10**6, transcendentals=0),
        name=kernel.__name__,
    )(*operands)


def swap_y(value, step):
    return lax.ppermute(value, "kern", [(i, i ^ (4 * step)) for i in range(16)])


def swap_z(value, step):
    return lax.ppermute(value, "kern", [(i, i ^ step) for i in range(16)])


def swap_inner(value):
    return lax.ppermute(value, "tile", [(i, i ^ 1) for i in range(16)])


def swap_outer(value):
    return lax.ppermute(value, "tile", [(i, ((i + 1) ^ 1) - 1 & 15) for i in range(16)])


def per_device(mask_field, target, kernel_spectra, kernel_weight):
    table = {name: jnp.asarray(value) for name, value in tables().items()}
    at_y = lax.axis_index("kern") // 4
    order = [pltpu.VMEM((4, HALF, 2 * SHARD), F32)]
    mask_field = mask_field.T
    inner, outer = swap_inner(mask_field), swap_outer(mask_field)
    heavy = call(weight_kernel, (8, 2 * SHARD), kernel_weight, smem=(0,))
    kernel_spectra, heavy = lax.optimization_barrier((kernel_spectra, heavy))
    kernels = [kernel_spectra] + [swap_y(kernel_spectra, step) for step in (1, 2, 3)]

    rows = call(
        window_kernel, (HALF, 2 * SHARD), outer, inner, mask_field, table["rows"], heavy
    )
    rows = [rows] + [swap_z(rows, step) for step in (1, 2, 3)]
    *rows, h1, h3 = lax.optimization_barrier((*rows, kernels[1], kernels[3]))
    kernels = [kernel_spectra, h1, kernels[2], h3]
    part = call(
        band_kernel, (2 * HALF, FREQS), *rows, table["band"]
    )
    parts = [part] + [swap_y(part, step) for step in (1, 2, 3)]
    field, image = call(
        aerial_kernel,
        [(COUNT * QUARTER, 2 * SAMPLES), (QUARTER, SAMPLES)],
        *parts, *kernels, table["unfold"], table["flip"], table["out"],
        table["pixels"], flops=4 * 10**9,
    )
    images = [image] + [swap_z(image, step) for step in (1, 2, 3)]
    goal = lax.dynamic_slice_in_dim(target, at_y * QUARTER, QUARTER, 0)
    messages = call(
        slope_kernel,
        [(2 * HALF + EXTRA, FREQS)] * 4,
        *images, goal, field, *kernels, table["spread"], table["spread_back"],
        table["pixels_back"], table["out_back"], table["flip_back"], table["fold"],
        scratch=[pltpu.VMEM((QUARTER, COLS), F32)],
    )
    messages = [messages[0]] + [swap_y(messages[step], step) for step in (1, 2, 3)]
    resist = call(resist_kernel, (SHARD, TILE), *messages)
    grads = call(
        columns_kernel,
        [(HALF, 2 * SHARD)] * 4,
        *messages, table["band_back"], table["edge_back"], scratch=order,
    )
    grad = grads[0]
    for step in (1, 2, 3):
        grad = grad + swap_z(grads[step], step)
    mask_grad = call(
        final_kernel, (SHARD, TILE), swap_inner(grad), swap_outer(grad), grad,
        table["rows"],
    )
    return (resist.T, mask_grad.T)


def solution(mesh):
    in_specs = (P("tile", "kern"), P("tile", None), P("kern", None, None, None), P("kern"))
    out_specs = (P("tile", "kern"), P("tile", "kern"))
    return jax.shard_map(
        per_device, mesh=mesh, in_specs=in_specs, out_specs=out_specs, check_vma=False
    )
```

```python
import math

import jax
import jax.numpy as jnp
import ml_dtypes
import numpy as np
from jax import lax
from jax.experimental import pallas as pl
from jax.experimental.pallas import tpu as pltpu
from jax.sharding import PartitionSpec as P

COLS = 1024
HALO = 128
FREQS = 128
TILE = 256
WINDOW = 512
SHARD = 64
SAMPLES = 256
QUARTER = 64
COUNT = 8
HALF = 72
EDGE_ROW = 65
WEIGHT_ROW = 67
EXTRA = 32
WIDE = 4 * SHARD
STEEPNESS = 4.0
THRESHOLD = 1.0
F32 = jnp.float32
BF16 = jnp.bfloat16


def angles(places, frequencies, length):
    return (np.outer(places, frequencies) % length) * (2.0 * math.pi / length)


def split_table(value):
    value = value.astype(np.float32)
    high = value.astype(ml_dtypes.bfloat16)
    low = (value - high.astype(np.float32)).astype(ml_dtypes.bfloat16)
    return np.stack([high, low])


def tables():
    freq = np.arange(FREQS) - FREQS // 2
    scale = 1.0 / math.sqrt(WINDOW * COLS)
    win = angles(np.arange(FREQS // 2 + 1), HALO + np.arange(TILE), WINDOW)
    rows = np.zeros((2, HALF, TILE))
    rows[0, : FREQS // 2 + 1] = np.cos(win) * scale
    rows[1, : FREQS // 2 + 1] = np.sin(win) * scale
    rows = rows.reshape(2 * HALF, TILE)
    col = angles(np.arange(COLS), freq, COLS)
    keep = FREQS // 2
    band = np.concatenate([np.cos(col[:, keep:]), np.sin(col[:, keep:])], 1)
    band[:, keep] = np.cos(col[:, 0])
    edge = np.sin(col[:, 0])
    wide = np.zeros((COLS // SHARD, SHARD, 2 * FREQS))
    wide[:, :, :FREQS] = band.reshape(COLS // SHARD, SHARD, FREQS)
    wide[:, :, FREQS] = edge.reshape(COLS // SHARD, SHARD)
    unfold = np.zeros((FREQS, 2 * FREQS))
    for place, value in enumerate(freq):
        size = abs(value)
        unfold[size, place] = 1.0
        if 0 < size < keep:
            unfold[keep + size, FREQS + place] = np.sign(value)
    flip = np.zeros((FREQS // 2, HALF))
    flip[np.arange(FREQS // 2), FREQS // 2 - np.arange(FREQS // 2)] = 1.0
    out = angles(HALO + np.arange(TILE), freq, WINDOW).reshape(4, QUARTER, FREQS)
    out_rows = np.concatenate([np.cos(out), np.sin(out)], 1) / FREQS
    pix = angles(freq, np.arange(SAMPLES), SAMPLES)
    pix_cos, pix_sin = np.cos(pix), np.sin(pix)
    pixels = np.concatenate(
        [np.concatenate([pix_cos, pix_sin], 1), np.concatenate([-pix_sin, pix_cos], 1)], 0
    )
    gap = np.arange(COLS)[None, :] - (COLS // SAMPLES) * np.arange(SAMPLES)[:, None]
    waves = np.arange(1, SAMPLES // 2)
    base = 2.0 * math.pi / COLS
    line = (1.0 + 2.0 * np.cos(base * np.outer(np.arange(COLS), waves)).sum(1)) / SAMPLES
    spread = line[gap % COLS]
    return {
        "rows": split_table(rows),
        "band": split_table(wide),
        "band_back": split_table(band.T),
        "edge_back": np.tile(edge, (8, 1)).astype(np.float32),
        "unfold": unfold.astype(ml_dtypes.bfloat16),
        "fold": unfold.T.astype(ml_dtypes.bfloat16),
        "flip": flip.astype(ml_dtypes.bfloat16),
        "flip_back": flip.T.astype(ml_dtypes.bfloat16),
        "out": split_table(out_rows),
        "out_back": split_table(out_rows.transpose(0, 2, 1)),
        "pixels": split_table(pixels),
        "pixels_back": split_table(pixels.T),
        "spread": split_table(spread),
        "spread_back": split_table(spread.T),
    }


def split(value):
    high = value.astype(BF16)
    low = (value - high.astype(F32)).astype(BF16)
    return high, low


def dot(former, latter):
    return lax.dot_general(
        former, latter, (((1,), (0,)), ((), ())), preferred_element_type=F32
    )


def dot_last(former, latter):
    return lax.dot_general(
        former, latter, (((1,), (1,)), ((), ())), preferred_element_type=F32
    )


def dot3(former, latter, dot=dot):
    return (
        dot(former[0], latter[0]) + dot(former[0], latter[1]) + dot(former[1], latter[0])
    )


def dot3_deep(former, latter):
    twice = jnp.concatenate([former[0], former[0]], 1)
    return dot(twice, jnp.concatenate(latter, 0)) + dot(former[1], latter[0])


def pair(ref):
    return ref[0], ref[1]


def moved(flip, value):
    high, low = split(value)
    return dot(flip, high) + dot(flip, low)


def moved_right(value, flip):
    high, low = split(value)
    return dot(high, flip) + dot(low, flip)


def pair_up(value):
    return jnp.concatenate([value[:HALF], value[HALF:]], 1)


def alternate(shape):
    return 1.0 - 2.0 * (lax.broadcasted_iota(jnp.int32, shape, 0) % 2).astype(F32)


def weight_kernel(weight_ref, out_ref):
    row = lax.broadcasted_iota(jnp.int32, out_ref.shape, 0)
    out_ref[...] = jnp.where(row == WEIGHT_ROW - HALF + 8, weight_ref[0], weight_ref[1])


def neighbours(outer, inner):
    tile = lax.axis_index("tile")
    last = lax.axis_size("tile") - 1
    outer = jnp.where((tile > 0) & (tile < last), outer, 0.0)
    odd = tile % 2 == 1
    return jnp.where(odd, inner, outer), jnp.where(odd, outer, inner)


def window_kernel(outer_ref, inner_ref, mask_ref, rows_ref, heavy_ref, out_ref):
    above, below = neighbours(outer_ref[...], inner_ref[...])
    above, below = above[:, TILE - HALO :], below[:, :HALO]
    sides = jnp.concatenate([below, above], 1)
    both = split(jnp.concatenate([mask_ref[...], sides], 0))
    done = dot3(pair(rows_ref), both, dot_last)
    own, halo = done[:, :SHARD], done[:, SHARD:]
    done = pair_up(own) + alternate((HALF, 2 * SHARD)) * pair_up(halo)
    row = lax.broadcasted_iota(jnp.int32, (8, 2 * SHARD), 0) + HALF - 8
    out_ref[: HALF - 8] = done[: HALF - 8]
    out_ref[HALF - 8 :] = jnp.where(row < WEIGHT_ROW, done[HALF - 8 :], heavy_ref[...])


def padded(row):
    return jnp.concatenate([row, jnp.zeros((1, FREQS - HALF), F32)], 1)


def with_edges(value, edges, weights=None):
    row = lax.broadcasted_iota(jnp.int32, value.shape, 0)
    for slot, edge in enumerate(edges):
        value = jnp.where(row == EDGE_ROW + slot, padded(edge), value)
    if weights is None:
        return value
    heavy = jnp.concatenate([value[: HALF - 8], weights, value[HALF:]], 0)
    return jnp.where((row >= WEIGHT_ROW) & (row < HALF), heavy, value)


def edge_columns(value):
    columns = value[HALF - 8 : HALF].T[:HALF]
    first = EDGE_ROW - (HALF - 8)
    return jnp.concatenate([columns[:, first : first + 1], columns[:, first + 1 : first + 2]], 0)


def band_kernel(r0, r1, r2, r3, band_ref, out_ref):
    kern = lax.axis_index("kern")
    at_y, at_z = kern // 4, kern % 4
    blocks = [ref[...] for ref in (r0, r1, r2, r3)]
    cos = jnp.concatenate([block[:, :SHARD] for block in blocks], 1)
    sin = jnp.concatenate([block[:, SHARD:] for block in blocks], 1)
    places = [4 * at_y + (at_z ^ step) for step in range(4)]
    band = tuple(
        jnp.concatenate([band_ref[i, pl.ds(place, 1)][0] for place in places], 0)
        for i in range(2)
    )
    done = dot3(split(jnp.concatenate([cos, sin], 0)), band)
    edges = [done[half : half + HALF, FREQS:].T[:1] for half in (0, HALF)]
    out_ref[...] = with_edges(done[:, :FREQS], edges, r0[HALF - 8 :])


def aerial_kernel(
    p0, p1, p2, p3, h0, h1, h2, h3, unfold_ref, flip_ref, out_rows_ref, pixels_ref,
    field_ref, image_ref,
):
    at_y = lax.axis_index("kern") // 4
    total = (p0[...] + p1[...]) + (p2[...] + p3[...])
    done = moved_right(total, unfold_ref[...])
    lane = lax.broadcasted_iota(jnp.int32, done.shape, 1)
    done = jnp.where(lane == FREQS, edge_columns(total), done)
    cos_cos, cos_sin = done[:HALF, :FREQS], done[:HALF, FREQS:]
    sin_cos, sin_sin = done[HALF:, :FREQS], done[HALF:, FREQS:]
    plus = jnp.concatenate([cos_cos - sin_sin, -(cos_sin + sin_cos)], 1)
    minus = jnp.concatenate([cos_cos + sin_sin, sin_cos - cos_sin], 1)
    spectrum = jnp.concatenate([moved(flip_ref[...], minus), plus[: FREQS // 2]], 0)
    spec_re, spec_im = spectrum[:, :FREQS], spectrum[:, FREQS:]
    out_rows = (
        out_rows_ref[0, pl.ds(at_y, 1)][0],
        out_rows_ref[1, pl.ds(at_y, 1)][0],
    )
    mids = []
    weights = []
    for part_ref, kernel_ref in zip((p0, p1, p2, p3), (h0, h1, h2, h3)):
        for slot in range(2):
            kern_re, kern_im = kernel_ref[slot, 0], kernel_ref[slot, 1]
            row = WEIGHT_ROW + slot
            weights.append(part_ref[row : row + 1, :1])
            band = jnp.concatenate(
                [
                    kern_re * spec_re - kern_im * spec_im,
                    kern_re * spec_im + kern_im * spec_re,
                ],
                1,
            )
            quads = dot3_deep(out_rows, split(band))
            upper, lower = quads[:QUARTER], quads[QUARTER:]
            mids.append(
                jnp.concatenate(
                    [
                        upper[:, :FREQS] - lower[:, FREQS:],
                        upper[:, FREQS:] + lower[:, :FREQS],
                    ],
                    1,
                )
            )
    field = dot3(split(jnp.concatenate(mids, 0)), pair(pixels_ref))
    image = None
    for slot in range(COUNT):
        part = field[slot * QUARTER : (slot + 1) * QUARTER]
        heavy = part * weights[slot]
        field_ref[slot * QUARTER : (slot + 1) * QUARTER, :] = heavy
        part = part * heavy
        part = part[:, :SAMPLES] + part[:, SAMPLES:]
        image = part if image is None else image + part
    image_ref[...] = image


def slope_kernel(
    i0, i1, i2, i3, goal_ref, field_ref, h0, h1, h2, h3,
    spread_ref, spread_back_ref, pixels_back_ref, out_back_ref, flip_back_ref,
    fold_ref, m0, m1, m2, m3, resist_ref,
):
    kern = lax.axis_index("kern")
    at_y, at_z = kern // 4, kern % 4
    image = (i0[...] + i1[...]) + (i2[...] + i3[...])
    image = dot3(split(image), pair(spread_ref))
    resist = 1.0 / (1.0 + jnp.exp(-STEEPNESS * (image - THRESHOLD)))
    goal = goal_ref[...].astype(F32)
    slope = 2.0 * STEEPNESS * (resist - goal) * resist * (1.0 - resist)
    slope = slope.astype(BF16)
    slope = dot(slope, spread_back_ref[0]) + dot(slope, spread_back_ref[1])
    slope = jnp.concatenate([slope, slope], 1)
    freqs = []
    for first in range(0, COUNT, 2):
        weighted = jnp.concatenate(
            [
                slope * field_ref[slot * QUARTER : (slot + 1) * QUARTER, :]
                for slot in range(first, first + 2)
            ],
            0,
        )
        freqs.append(dot3(split(weighted), pair(pixels_back_ref)))
    freqs = jnp.concatenate(freqs, 0)
    out_back = (
        out_back_ref[0, pl.ds(at_y, 1)][0],
        out_back_ref[1, pl.ds(at_y, 1)][0],
    )
    grad_re = grad_im = None
    for slot in range(COUNT):
        kernel_ref = (h0, h1, h2, h3)[slot // 2]
        kern_re, kern_im = kernel_ref[slot % 2, 0], kernel_ref[slot % 2, 1]
        part = freqs[slot * QUARTER : (slot + 1) * QUARTER]
        block = jnp.concatenate(
            [part, jnp.concatenate([part[:, FREQS:], -part[:, :FREQS]], 1)], 0
        )
        adjoint = dot3_deep(out_back, split(block))
        adj_re, adj_im = adjoint[:, :FREQS], adjoint[:, FREQS:]
        term_re = kern_re * adj_re + kern_im * adj_im
        term_im = kern_re * adj_im - kern_im * adj_re
        grad_re = term_re if grad_re is None else grad_re + term_re
        grad_im = term_im if grad_im is None else grad_im + term_im
    grad = jnp.concatenate([grad_re, grad_im], 1)
    plus = jnp.concatenate(
        [grad[FREQS // 2 :], jnp.zeros((HALF - FREQS // 2, 2 * FREQS), F32)], 0
    )
    minus = moved(flip_back_ref[...], grad[: FREQS // 2])
    both, less = plus + minus, minus - plus
    done = jnp.concatenate(
        [
            jnp.concatenate([both[:, :FREQS], -both[:, FREQS:]], 1),
            jnp.concatenate([less[:, FREQS:], less[:, :FREQS]], 1),
        ],
        0,
    )
    first = done[:, FREQS : FREQS + 8].T[:1]
    done = moved_right(done, fold_ref[...])
    done = with_edges(done, (first[:, :HALF], first[:, HALF:]))
    resist_ref[...] = resist
    for step, message in enumerate((m0, m1, m2, m3)):
        message[: 2 * HALF, :] = done
        block = 4 * (at_y ^ step) + at_z
        start = pl.multiple_of((block // 2) * 2 * SHARD, 2 * SHARD)
        wide = resist_ref[:, pl.ds(start, 2 * SHARD)].T
        piece = jnp.where(block % 2 == 0, wide[:SHARD], wide[SHARD:])
        message[2 * HALF :, :] = jnp.concatenate([piece[:EXTRA], piece[EXTRA:]], 1)


def columns_kernel(
    m0, m1, m2, m3, band_back_ref, edge_ref, g0, g1, g2, g3, order_ref
):
    kern = lax.axis_index("kern")
    at_y, at_z = kern // 4, kern % 4
    rows = slice(0, 2 * HALF)
    total = (m0[rows] + m1[rows]) + (m2[rows] + m3[rows])
    start = pl.multiple_of(at_y * WIDE, WIDE)
    band = tuple(band_back_ref[i, :, pl.ds(start, WIDE)] for i in range(2))
    done = dot3(split(total), band)
    done = done + edge_columns(total) * edge_ref[:1, pl.ds(start, WIDE)]
    for slot in range(4):
        cols = slice(slot * SHARD, (slot + 1) * SHARD)
        order_ref[slot] = jnp.concatenate([done[:HALF, cols], done[HALF:, cols]], 1)
    for step, out in enumerate((g0, g1, g2, g3)):
        out[...] = order_ref[pl.ds(at_z ^ step, 1)][0]


def resist_kernel(m0, m1, m2, m3, resist_ref):
    at_y = lax.axis_index("kern") // 4
    pieces = []
    for message in (m0, m1, m2, m3):
        piece = message[2 * HALF :, :]
        pieces.append(jnp.concatenate([piece[:, :SHARD], piece[:, SHARD:]], 0))
    spots = []
    for slot in range(4):
        spot = pieces[0]
        for step in (1, 2, 3):
            spot = jnp.where((at_y ^ step) == slot, pieces[step], spot)
        spots.append(spot)
    resist_ref[...] = jnp.concatenate(spots, 1)


def final_kernel(inner_ref, outer_ref, own_ref, rows_ref, out_ref):
    above, below = neighbours(outer_ref[...], inner_ref[...])
    own = own_ref[...]
    sign = 2.0 * alternate(own.shape)
    own = 2.0 * own
    sides = (
        own + above * sign,
        own + below * sign,
    )
    for slot, side in enumerate(sides):
        side = split(side.T)
        cols = slice(slot * HALO, (slot + 1) * HALO)
        total = None
        for half in range(2):
            part = dot3(
                (side[0][half * SHARD : (half + 1) * SHARD], side[1][half * SHARD : (half + 1) * SHARD]),
                tuple(rows_ref[i, half * HALF : (half + 1) * HALF, cols] for i in range(2)),
            )
            total = part if total is None else total + part
        out_ref[:, cols] = total


def call(kernel, shapes, *operands, flops=4 * 10**9, smem=(), hbm=(), scratch=()):
    many = isinstance(shapes, list)
    space = lambda i: pltpu.SMEM if i in smem else pltpu.HBM if i in hbm else pltpu.VMEM
    spec = lambda i: pl.BlockSpec(memory_space=space(i))
    out = [jax.ShapeDtypeStruct(shape, F32) for shape in (shapes if many else [shapes])]
    return pl.pallas_call(
        kernel,
        scratch_shapes=list(scratch),
        out_shape=out if many else out[0],
        in_specs=[spec(i) for i in range(len(operands))],
        out_specs=[pl.BlockSpec(memory_space=pltpu.VMEM)] * len(out)
        if many
        else pl.BlockSpec(memory_space=pltpu.VMEM),
        compiler_params=pltpu.CompilerParams(vmem_limit_bytes=32 * 2**20),
        cost_estimate=pl.CostEstimate(flops=flops, bytes_accessed=10**6, transcendentals=0),
        name=kernel.__name__,
    )(*operands)


def swap_y(value, step):
    return lax.ppermute(value, "kern", [(i, i ^ (4 * step)) for i in range(16)])


def swap_z(value, step):
    return lax.ppermute(value, "kern", [(i, i ^ step) for i in range(16)])


def swap_inner(value):
    return lax.ppermute(value, "tile", [(i, i ^ 1) for i in range(16)])


def swap_outer(value):
    return lax.ppermute(value, "tile", [(i, ((i + 1) ^ 1) - 1 & 15) for i in range(16)])


def per_device(mask_field, target, kernel_spectra, kernel_weight):
    table = {name: jnp.asarray(value) for name, value in tables().items()}
    at_y = lax.axis_index("kern") // 4
    order = [pltpu.VMEM((4, HALF, 2 * SHARD), F32)]
    mask_field = mask_field.T
    inner, outer = swap_inner(mask_field), swap_outer(mask_field)
    heavy = call(weight_kernel, (8, 2 * SHARD), kernel_weight, smem=(0,))
    kernel_spectra, heavy = lax.optimization_barrier((kernel_spectra, heavy))
    kernels = [kernel_spectra] + [swap_y(kernel_spectra, step) for step in (1, 2, 3)]

    rows = call(
        window_kernel, (HALF, 2 * SHARD), outer, inner, mask_field, table["rows"], heavy
    )
    rows = [rows] + [swap_z(rows, step) for step in (1, 2, 3)]
    *rows, h1, h3 = lax.optimization_barrier((*rows, kernels[1], kernels[3]))
    kernels = [kernel_spectra, h1, kernels[2], h3]
    part = call(
        band_kernel, (2 * HALF, FREQS), *rows, table["band"]
    )
    near, far, middle = [swap_y(part, step) for step in (1, 3, 2)]
    parts = [part, near, middle, far]
    field, image = call(
        aerial_kernel,
        [(COUNT * QUARTER, 2 * SAMPLES), (QUARTER, SAMPLES)],
        *parts, *kernels, table["unfold"], table["flip"], table["out"],
        table["pixels"], flops=4 * 10**9,
    )
    images = [image] + [swap_z(image, step) for step in (1, 3, 2)]
    goal = lax.dynamic_slice_in_dim(target, at_y * QUARTER, QUARTER, 0)
    messages = call(
        slope_kernel,
        [(2 * HALF + EXTRA, FREQS)] * 4,
        *images, goal, field, *kernels, table["spread"], table["spread_back"],
        table["pixels_back"], table["out_back"], table["flip_back"], table["fold"],
        scratch=[pltpu.VMEM((QUARTER, COLS), F32)],
    )
    messages = [messages[0]] + [swap_y(messages[step], step) for step in (1, 2, 3)]
    resist = call(resist_kernel, (SHARD, TILE), *messages)
    grads = call(
        columns_kernel,
        [(HALF, 2 * SHARD)] * 4,
        *messages, table["band_back"], table["edge_back"], scratch=order,
    )
    grad = grads[0]
    for step in (1, 2, 3):
        grad = grad + swap_z(grads[step], step)
    mask_grad = call(
        final_kernel, (SHARD, TILE), swap_inner(grad), swap_outer(grad), grad,
        table["rows"],
    )
    return (resist.T, mask_grad.T)


def solution(mesh):
    in_specs = (P("tile", "kern"), P("tile", None), P("kern", None, None, None), P("kern"))
    out_specs = (P("tile", "kern"), P("tile", "kern"))
    return jax.shard_map(
        per_device, mesh=mesh, in_specs=in_specs, out_specs=out_specs, check_vma=False
    )
```

```python
import math

import jax
import jax.numpy as jnp
import ml_dtypes
import numpy as np
from jax import lax
from jax.experimental import pallas as pl
from jax.experimental.pallas import tpu as pltpu
from jax.sharding import PartitionSpec as P

COLS = 1024
HALO = 128
FREQS = 128
TILE = 256
WINDOW = 512
SHARD = 64
SAMPLES = 256
QUARTER = 64
COUNT = 8
HALF = 72
ROOM = 80
EDGE_ROW = 65
WEIGHT_ROW = 67
EXTRA = 32
WIDE = 4 * SHARD
STEEPNESS = 4.0
THRESHOLD = 1.0
F32 = jnp.float32
BF16 = jnp.bfloat16


def angles(places, frequencies, length):
    return (np.outer(places, frequencies) % length) * (2.0 * math.pi / length)


def split_table(value):
    value = value.astype(np.float32)
    high = value.astype(ml_dtypes.bfloat16)
    low = (value - high.astype(np.float32)).astype(ml_dtypes.bfloat16)
    return np.stack([high, low])


def split_table3(value):
    pair = split_table(value)
    rest = value - pair.astype(np.float64).sum(0)
    return np.concatenate([pair, rest.astype(ml_dtypes.bfloat16)[None]])


def tables():
    freq = np.arange(FREQS) - FREQS // 2
    scale = 1.0 / math.sqrt(WINDOW * COLS)
    win = angles(np.arange(FREQS // 2 + 1), HALO + np.arange(TILE), WINDOW)
    rows = np.zeros((2, ROOM, TILE))
    rows[0, : FREQS // 2 + 1] = np.cos(win) * scale
    rows[1, : FREQS // 2 + 1] = np.sin(win) * scale
    rows = rows.reshape(2 * ROOM, TILE)
    col = angles(np.arange(COLS), freq, COLS)
    keep = FREQS // 2
    band = np.concatenate([np.cos(col[:, keep:]), np.sin(col[:, keep:])], 1)
    band[:, keep] = np.cos(col[:, 0])
    edge = np.sin(col[:, 0])
    wide = np.zeros((COLS // SHARD, SHARD, 2 * FREQS))
    wide[:, :, :FREQS] = band.reshape(COLS // SHARD, SHARD, FREQS)
    wide[:, :, FREQS] = edge.reshape(COLS // SHARD, SHARD)
    unfold = np.zeros((FREQS, 2 * FREQS))
    for place, value in enumerate(freq):
        size = abs(value)
        unfold[size, place] = 1.0
        if 0 < size < keep:
            unfold[keep + size, FREQS + place] = np.sign(value)
    flip = np.zeros((FREQS // 2, HALF))
    flip[np.arange(FREQS // 2), FREQS // 2 - np.arange(FREQS // 2)] = 1.0
    out = angles(HALO + np.arange(TILE), freq, WINDOW).reshape(4, QUARTER, FREQS)
    out_rows = np.concatenate([np.cos(out), np.sin(out)], 1) / FREQS
    pix = angles(freq, np.arange(SAMPLES), SAMPLES)
    pix_cos, pix_sin = np.cos(pix), np.sin(pix)
    pixels = np.concatenate(
        [np.concatenate([pix_cos, pix_sin], 1), np.concatenate([-pix_sin, pix_cos], 1)], 0
    )
    gap = np.arange(COLS)[None, :] - (COLS // SAMPLES) * np.arange(SAMPLES)[:, None]
    waves = np.arange(1, SAMPLES // 2)
    base = 2.0 * math.pi / COLS
    line = (1.0 + 2.0 * np.cos(base * np.outer(np.arange(COLS), waves)).sum(1)) / SAMPLES
    spread = line[gap % COLS]
    return {
        "rows": split_table(rows),
        "band": split_table(wide),
        "band_back": split_table(band.T),
        "edge_back": np.tile(edge, (8, 1)).astype(np.float32),
        "unfold": unfold.astype(ml_dtypes.bfloat16),
        "fold": unfold.T.astype(ml_dtypes.bfloat16),
        "flip": flip.astype(ml_dtypes.bfloat16),
        "flip_back": flip.T.astype(ml_dtypes.bfloat16),
        "out": split_table(out_rows),
        "out_back": split_table(out_rows.transpose(0, 2, 1)),
        "pixels": split_table(pixels),
        "pixels_back": split_table(pixels.T),
        "spread": split_table3(spread),
        "spread_back": split_table(spread.T),
    }


def split(value):
    high = value.astype(BF16)
    low = (value - high.astype(F32)).astype(BF16)
    return high, low


def dot(former, latter):
    return lax.dot_general(
        former, latter, (((1,), (0,)), ((), ())), preferred_element_type=F32
    )


def dot_last(former, latter):
    return lax.dot_general(
        former, latter, (((1,), (1,)), ((), ())), preferred_element_type=F32
    )


def dot3(former, latter, dot=dot):
    return (
        dot(former[0], latter[0]) + dot(former[0], latter[1]) + dot(former[1], latter[0])
    )


def dot3_deep(former, latter):
    twice = jnp.concatenate([former[0], former[0]], 1)
    return dot(twice, jnp.concatenate(latter, 0)) + dot(former[1], latter[0])


def dot6(former, latter):
    high, mid = split(former)
    low = ((former - high.astype(F32)) - mid.astype(F32)).astype(BF16)
    count = former.shape[0]
    most = dot(jnp.concatenate([high, mid, low], 0), latter[0])
    some = dot(jnp.concatenate([high, mid], 0), latter[1])
    small = dot(high, latter[2]) + some[count:] + most[2 * count :]
    return small + some[:count] + most[count : 2 * count] + most[:count]


def pair(ref):
    return ref[0], ref[1]


def moved(flip, value):
    high, low = split(value)
    return dot(flip, high) + dot(flip, low)


def moved_right(value, flip):
    high, low = split(value)
    return dot(high, flip) + dot(low, flip)


def pair_up(value):
    return jnp.concatenate([value[:HALF], value[ROOM : ROOM + HALF]], 1)


def alternate(shape):
    return 1.0 - 2.0 * (lax.broadcasted_iota(jnp.int32, shape, 0) % 2).astype(F32)


def weight_kernel(weight_ref, out_ref):
    row = lax.broadcasted_iota(jnp.int32, out_ref.shape, 0)
    out_ref[...] = jnp.where(row == WEIGHT_ROW - HALF + 8, weight_ref[0], weight_ref[1])


def neighbours(outer, inner):
    tile = lax.axis_index("tile")
    last = lax.axis_size("tile") - 1
    outer = jnp.where((tile > 0) & (tile < last), outer, 0.0)
    odd = tile % 2 == 1
    return jnp.where(odd, inner, outer), jnp.where(odd, outer, inner)


def window_kernel(outer_ref, inner_ref, mask_ref, rows_ref, heavy_ref, out_ref):
    above, below = neighbours(outer_ref[...], inner_ref[...])
    above, below = above[:, TILE - HALO :], below[:, :HALO]
    sides = jnp.concatenate([below, above], 1)
    both = split(jnp.concatenate([mask_ref[...], sides], 0))
    done = dot3(pair(rows_ref), both, dot_last)
    own, halo = done[:, :SHARD], done[:, SHARD:]
    done = pair_up(own) + alternate((HALF, 2 * SHARD)) * pair_up(halo)
    row = lax.broadcasted_iota(jnp.int32, (8, 2 * SHARD), 0) + HALF - 8
    out_ref[: HALF - 8] = done[: HALF - 8]
    out_ref[HALF - 8 :] = jnp.where(row < WEIGHT_ROW, done[HALF - 8 :], heavy_ref[...])


def padded(row):
    return jnp.concatenate([row, jnp.zeros((1, FREQS - HALF), F32)], 1)


def with_edges(value, edges, weights=None):
    row = lax.broadcasted_iota(jnp.int32, value.shape, 0)
    for slot, edge in enumerate(edges):
        value = jnp.where(row == EDGE_ROW + slot, padded(edge), value)
    if weights is None:
        return value
    heavy = jnp.concatenate([value[: HALF - 8], weights, value[HALF:]], 0)
    return jnp.where((row >= WEIGHT_ROW) & (row < HALF), heavy, value)


def edge_columns(value):
    columns = value[HALF - 8 : HALF].T[:HALF]
    first = EDGE_ROW - (HALF - 8)
    return jnp.concatenate([columns[:, first : first + 1], columns[:, first + 1 : first + 2]], 0)


def band_kernel(r0, r1, r2, r3, band_ref, out_ref):
    kern = lax.axis_index("kern")
    at_y, at_z = kern // 4, kern % 4
    blocks = [ref[...] for ref in (r0, r1, r2, r3)]
    cos = jnp.concatenate([block[:, :SHARD] for block in blocks], 1)
    sin = jnp.concatenate([block[:, SHARD:] for block in blocks], 1)
    places = [4 * at_y + (at_z ^ step) for step in range(4)]
    band = tuple(
        jnp.concatenate([band_ref[i, pl.ds(place, 1)][0] for place in places], 0)
        for i in range(2)
    )
    done = dot3(split(jnp.concatenate([cos, sin], 0)), band)
    edges = [done[half : half + HALF, FREQS:].T[:1] for half in (0, HALF)]
    out_ref[...] = with_edges(done[:, :FREQS], edges, r0[HALF - 8 :])


def aerial_kernel(
    p0, p1, p2, p3, h0, h1, h2, h3, unfold_ref, flip_ref, out_rows_ref, pixels_ref,
    field_ref, image_ref,
):
    at_y = lax.axis_index("kern") // 4
    total = (p0[...] + p1[...]) + (p2[...] + p3[...])
    done = moved_right(total, unfold_ref[...])
    lane = lax.broadcasted_iota(jnp.int32, done.shape, 1)
    done = jnp.where(lane == FREQS, edge_columns(total), done)
    cos_cos, cos_sin = done[:HALF, :FREQS], done[:HALF, FREQS:]
    sin_cos, sin_sin = done[HALF:, :FREQS], done[HALF:, FREQS:]
    plus = jnp.concatenate([cos_cos - sin_sin, -(cos_sin + sin_cos)], 1)
    minus = jnp.concatenate([cos_cos + sin_sin, sin_cos - cos_sin], 1)
    spectrum = jnp.concatenate([moved(flip_ref[...], minus), plus[: FREQS // 2]], 0)
    spec_re, spec_im = spectrum[:, :FREQS], spectrum[:, FREQS:]
    out_rows = (
        out_rows_ref[0, pl.ds(at_y, 1)][0],
        out_rows_ref[1, pl.ds(at_y, 1)][0],
    )
    mids = []
    weights = []
    for part_ref, kernel_ref in zip((p0, p1, p2, p3), (h0, h1, h2, h3)):
        for slot in range(2):
            kern_re, kern_im = kernel_ref[slot, 0], kernel_ref[slot, 1]
            row = WEIGHT_ROW + slot
            weights.append(part_ref[row : row + 1, :1])
            band = jnp.concatenate(
                [
                    kern_re * spec_re - kern_im * spec_im,
                    kern_re * spec_im + kern_im * spec_re,
                ],
                1,
            )
            quads = dot3_deep(out_rows, split(band))
            upper, lower = quads[:QUARTER], quads[QUARTER:]
            mids.append(
                jnp.concatenate(
                    [
                        upper[:, :FREQS] - lower[:, FREQS:],
                        upper[:, FREQS:] + lower[:, :FREQS],
                    ],
                    1,
                )
            )
    field = dot3(split(jnp.concatenate(mids, 0)), pair(pixels_ref))
    image = None
    for slot in range(COUNT):
        part = field[slot * QUARTER : (slot + 1) * QUARTER]
        heavy = part * weights[slot]
        field_ref[slot * QUARTER : (slot + 1) * QUARTER, :] = heavy
        part = part * heavy
        part = part[:, :SAMPLES] + part[:, SAMPLES:]
        image = part if image is None else image + part
    image_ref[...] = image


def slope_kernel(
    i0, i1, i2, i3, goal_ref, field_ref, h0, h1, h2, h3,
    spread_ref, spread_back_ref, pixels_back_ref, out_back_ref, flip_back_ref,
    fold_ref, m0, m1, m2, m3, resist_ref,
):
    kern = lax.axis_index("kern")
    at_y, at_z = kern // 4, kern % 4
    image = (i0[...] + i1[...]) + (i2[...] + i3[...])
    image = dot6(image, spread_ref)
    resist = 1.0 / (1.0 + jnp.exp(-STEEPNESS * (image - THRESHOLD)))
    goal = goal_ref[...].astype(F32)
    slope = 2.0 * STEEPNESS * (resist - goal) * resist * (1.0 - resist)
    slope = slope.astype(BF16)
    slope = dot(slope, spread_back_ref[0]) + dot(slope, spread_back_ref[1])
    slope = jnp.concatenate([slope, slope], 1)
    freqs = []
    for first in range(0, COUNT, 2):
        weighted = jnp.concatenate(
            [
                slope * field_ref[slot * QUARTER : (slot + 1) * QUARTER, :]
                for slot in range(first, first + 2)
            ],
            0,
        )
        freqs.append(dot3(split(weighted), pair(pixels_back_ref)))
    freqs = jnp.concatenate(freqs, 0)
    out_back = (
        out_back_ref[0, pl.ds(at_y, 1)][0],
        out_back_ref[1, pl.ds(at_y, 1)][0],
    )
    grad_re = grad_im = None
    for slot in range(COUNT):
        kernel_ref = (h0, h1, h2, h3)[slot // 2]
        kern_re, kern_im = kernel_ref[slot % 2, 0], kernel_ref[slot % 2, 1]
        part = freqs[slot * QUARTER : (slot + 1) * QUARTER]
        block = jnp.concatenate(
            [part, jnp.concatenate([part[:, FREQS:], -part[:, :FREQS]], 1)], 0
        )
        adjoint = dot3_deep(out_back, split(block))
        adj_re, adj_im = adjoint[:, :FREQS], adjoint[:, FREQS:]
        term_re = kern_re * adj_re + kern_im * adj_im
        term_im = kern_re * adj_im - kern_im * adj_re
        grad_re = term_re if grad_re is None else grad_re + term_re
        grad_im = term_im if grad_im is None else grad_im + term_im
    grad = jnp.concatenate([grad_re, grad_im], 1)
    plus = jnp.concatenate(
        [grad[FREQS // 2 :], jnp.zeros((HALF - FREQS // 2, 2 * FREQS), F32)], 0
    )
    minus = moved(flip_back_ref[...], grad[: FREQS // 2])
    both, less = plus + minus, minus - plus
    done = jnp.concatenate(
        [
            jnp.concatenate([both[:, :FREQS], -both[:, FREQS:]], 1),
            jnp.concatenate([less[:, FREQS:], less[:, :FREQS]], 1),
        ],
        0,
    )
    first = done[:, FREQS : FREQS + 8].T[:1]
    done = moved_right(done, fold_ref[...])
    done = with_edges(done, (first[:, :HALF], first[:, HALF:]))
    resist_ref[...] = resist
    for step, message in enumerate((m0, m1, m2, m3)):
        message[: 2 * HALF, :] = done
        block = 4 * (at_y ^ step) + at_z
        start = pl.multiple_of((block // 2) * 2 * SHARD, 2 * SHARD)
        wide = resist_ref[:, pl.ds(start, 2 * SHARD)].T
        piece = jnp.where(block % 2 == 0, wide[:SHARD], wide[SHARD:])
        message[2 * HALF :, :] = jnp.concatenate([piece[:EXTRA], piece[EXTRA:]], 1)


def columns_kernel(
    m0, m1, m2, m3, band_back_ref, edge_ref, g0, g1, g2, g3, order_ref
):
    kern = lax.axis_index("kern")
    at_y, at_z = kern // 4, kern % 4
    rows = slice(0, 2 * HALF)
    total = (m0[rows] + m1[rows]) + (m2[rows] + m3[rows])
    start = pl.multiple_of(at_y * WIDE, WIDE)
    band = tuple(band_back_ref[i, :, pl.ds(start, WIDE)] for i in range(2))
    done = dot3(split(total), band)
    done = done + edge_columns(total) * edge_ref[:1, pl.ds(start, WIDE)]
    for slot in range(4):
        cols = slice(slot * SHARD, (slot + 1) * SHARD)
        order_ref[slot] = jnp.concatenate([done[:HALF, cols], done[HALF:, cols]], 1)
    for step, out in enumerate((g0, g1, g2, g3)):
        out[...] = order_ref[pl.ds(at_z ^ step, 1)][0]


def resist_kernel(m0, m1, m2, m3, resist_ref):
    at_y = lax.axis_index("kern") // 4
    pieces = []
    for message in (m0, m1, m2, m3):
        piece = message[2 * HALF :, :]
        pieces.append(jnp.concatenate([piece[:, :SHARD], piece[:, SHARD:]], 0))
    spots = []
    for slot in range(4):
        spot = pieces[0]
        for step in (1, 2, 3):
            spot = jnp.where((at_y ^ step) == slot, pieces[step], spot)
        spots.append(spot)
    resist_ref[...] = jnp.concatenate(spots, 1)


def final_kernel(inner_ref, outer_ref, own_ref, rows_ref, out_ref):
    above, below = neighbours(outer_ref[...], inner_ref[...])
    own = own_ref[...]
    sign = 2.0 * alternate(own.shape)
    own = 2.0 * own
    sides = (
        own + above * sign,
        own + below * sign,
    )
    for slot, side in enumerate(sides):
        side = split(jnp.concatenate([side, jnp.zeros((ROOM - HALF, 2 * SHARD), F32)], 0).T)
        cols = slice(slot * HALO, (slot + 1) * HALO)
        total = None
        for half in range(2):
            part = dot3(
                (side[0][half * SHARD : (half + 1) * SHARD], side[1][half * SHARD : (half + 1) * SHARD]),
                tuple(rows_ref[i, half * ROOM : (half + 1) * ROOM, cols] for i in range(2)),
            )
            total = part if total is None else total + part
        out_ref[:, cols] = total


def call(kernel, shapes, *operands, flops=4 * 10**9, smem=(), hbm=(), scratch=()):
    many = isinstance(shapes, list)
    space = lambda i: pltpu.SMEM if i in smem else pltpu.HBM if i in hbm else pltpu.VMEM
    spec = lambda i: pl.BlockSpec(memory_space=space(i))
    out = [jax.ShapeDtypeStruct(shape, F32) for shape in (shapes if many else [shapes])]
    return pl.pallas_call(
        kernel,
        scratch_shapes=list(scratch),
        out_shape=out if many else out[0],
        in_specs=[spec(i) for i in range(len(operands))],
        out_specs=[pl.BlockSpec(memory_space=pltpu.VMEM)] * len(out)
        if many
        else pl.BlockSpec(memory_space=pltpu.VMEM),
        compiler_params=pltpu.CompilerParams(vmem_limit_bytes=32 * 2**20),
        cost_estimate=pl.CostEstimate(flops=flops, bytes_accessed=10**6, transcendentals=0),
        name=kernel.__name__,
    )(*operands)


def swap_y(value, step):
    return lax.ppermute(value, "kern", [(i, i ^ (4 * step)) for i in range(16)])


def swap_z(value, step):
    return lax.ppermute(value, "kern", [(i, i ^ step) for i in range(16)])


def swap_inner(value):
    return lax.ppermute(value, "tile", [(i, i ^ 1) for i in range(16)])


def swap_outer(value):
    return lax.ppermute(value, "tile", [(i, ((i + 1) ^ 1) - 1 & 15) for i in range(16)])


def per_device(mask_field, target, kernel_spectra, kernel_weight):
    table = {name: jnp.asarray(value) for name, value in tables().items()}
    at_y = lax.axis_index("kern") // 4
    order = [pltpu.VMEM((4, HALF, 2 * SHARD), F32)]
    mask_field = mask_field.T
    inner, outer = swap_inner(mask_field), swap_outer(mask_field)
    heavy = call(weight_kernel, (8, 2 * SHARD), kernel_weight, smem=(0,))
    kernel_spectra, heavy = lax.optimization_barrier((kernel_spectra, heavy))
    kernels = [kernel_spectra] + [swap_y(kernel_spectra, step) for step in (1, 2, 3)]

    rows = call(
        window_kernel, (HALF, 2 * SHARD), outer, inner, mask_field, table["rows"], heavy
    )
    rows = [rows] + [swap_z(rows, step) for step in (1, 2, 3)]
    *rows, h1, h3 = lax.optimization_barrier((*rows, kernels[1], kernels[3]))
    kernels = [kernel_spectra, h1, kernels[2], h3]
    part = call(
        band_kernel, (2 * HALF, FREQS), *rows, table["band"]
    )
    near, far, middle = [swap_y(part, step) for step in (1, 3, 2)]
    parts = [part, near, middle, far]
    field, image = call(
        aerial_kernel,
        [(COUNT * QUARTER, 2 * SAMPLES), (QUARTER, SAMPLES)],
        *parts, *kernels, table["unfold"], table["flip"], table["out"],
        table["pixels"], flops=4 * 10**9,
    )
    images = [image] + [swap_z(image, step) for step in (1, 3, 2)]
    goal = lax.dynamic_slice_in_dim(target, at_y * QUARTER, QUARTER, 0)
    messages = call(
        slope_kernel,
        [(2 * HALF + EXTRA, FREQS)] * 4,
        *images, goal, field, *kernels, table["spread"], table["spread_back"],
        table["pixels_back"], table["out_back"], table["flip_back"], table["fold"],
        scratch=[pltpu.VMEM((QUARTER, COLS), F32)],
    )
    messages = [messages[0]] + [swap_y(messages[step], step) for step in (1, 2, 3)]
    resist = call(resist_kernel, (SHARD, TILE), *messages)
    grads = call(
        columns_kernel,
        [(HALF, 2 * SHARD)] * 4,
        *messages, table["band_back"], table["edge_back"], scratch=order,
    )
    grad = grads[0]
    for step in (1, 2, 3):
        grad = grad + swap_z(grads[step], step)
    mask_grad = call(
        final_kernel, (SHARD, TILE), swap_inner(grad), swap_outer(grad), grad,
        table["rows"],
    )
    return (resist.T, mask_grad.T)


def solution(mesh):
    in_specs = (P("tile", "kern"), P("tile", None), P("kern", None, None, None), P("kern"))
    out_specs = (P("tile", "kern"), P("tile", "kern"))
    return jax.shard_map(
        per_device, mesh=mesh, in_specs=in_specs, out_specs=out_specs, check_vma=False
    )
```

```python
import math

import jax
import jax.numpy as jnp
import ml_dtypes
import numpy as np
from jax import lax
from jax.experimental import pallas as pl
from jax.experimental.pallas import tpu as pltpu
from jax.sharding import PartitionSpec as P

COLS = 1024
HALO = 128
FREQS = 128
TILE = 256
WINDOW = 512
SHARD = 64
SAMPLES = 256
QUARTER = 64
COUNT = 8
HALF = 72
ROOM = 80
EDGE_ROW = 65
WEIGHT_ROW = 67
EXTRA = 32
WIDE = 4 * SHARD
STEEPNESS = 4.0
THRESHOLD = 1.0
F32 = jnp.float32
BF16 = jnp.bfloat16


def angles(places, frequencies, length):
    return (np.outer(places, frequencies) % length) * (2.0 * math.pi / length)


def split_table(value):
    value = value.astype(np.float32)
    high = value.astype(ml_dtypes.bfloat16)
    low = (value - high.astype(np.float32)).astype(ml_dtypes.bfloat16)
    return np.stack([high, low])


def split_table3(value):
    pair = split_table(value)
    rest = value - pair.astype(np.float64).sum(0)
    return np.concatenate([pair, rest.astype(ml_dtypes.bfloat16)[None]])


def tables():
    freq = np.arange(FREQS) - FREQS // 2
    scale = 1.0 / math.sqrt(WINDOW * COLS)
    win = angles(np.arange(FREQS // 2 + 1), HALO + np.arange(TILE), WINDOW)
    rows = np.zeros((2, ROOM, TILE))
    rows[0, : FREQS // 2 + 1] = np.cos(win) * scale
    rows[1, : FREQS // 2 + 1] = np.sin(win) * scale
    rows = rows.reshape(2 * ROOM, TILE)
    col = angles(np.arange(COLS), freq, COLS)
    keep = FREQS // 2
    band = np.concatenate([np.cos(col[:, keep:]), np.sin(col[:, keep:])], 1)
    band[:, keep] = np.cos(col[:, 0])
    edge = np.sin(col[:, 0])
    wide = np.zeros((COLS // SHARD, SHARD, 2 * FREQS))
    wide[:, :, :FREQS] = band.reshape(COLS // SHARD, SHARD, FREQS)
    wide[:, :, FREQS] = edge.reshape(COLS // SHARD, SHARD)
    unfold = np.zeros((FREQS, 2 * FREQS))
    for place, value in enumerate(freq):
        size = abs(value)
        unfold[size, place] = 1.0
        if 0 < size < keep:
            unfold[keep + size, FREQS + place] = np.sign(value)
    flip = np.zeros((FREQS // 2, HALF))
    flip[np.arange(FREQS // 2), FREQS // 2 - np.arange(FREQS // 2)] = 1.0
    out = angles(HALO + np.arange(TILE), freq, WINDOW).reshape(4, QUARTER, FREQS)
    out_rows = np.concatenate([np.cos(out), np.sin(out)], 1) / FREQS
    pix = angles(freq, np.arange(SAMPLES), SAMPLES)
    pix_cos, pix_sin = np.cos(pix), np.sin(pix)
    pixels = np.concatenate(
        [np.concatenate([pix_cos, pix_sin], 1), np.concatenate([-pix_sin, pix_cos], 1)], 0
    )
    gap = np.arange(COLS)[None, :] - (COLS // SAMPLES) * np.arange(SAMPLES)[:, None]
    waves = np.arange(1, SAMPLES // 2)
    base = 2.0 * math.pi / COLS
    line = (1.0 + 2.0 * np.cos(base * np.outer(np.arange(COLS), waves)).sum(1)) / SAMPLES
    spread = line[gap % COLS]
    return {
        "rows": split_table(rows),
        "band": split_table(wide),
        "band_back": split_table(band.T),
        "edge_back": np.tile(edge, (8, 1)).astype(np.float32),
        "unfold": unfold.astype(ml_dtypes.bfloat16),
        "fold": unfold.T.astype(ml_dtypes.bfloat16),
        "flip": flip.astype(ml_dtypes.bfloat16),
        "flip_back": flip.T.astype(ml_dtypes.bfloat16),
        "out": split_table(out_rows),
        "out_back": split_table(out_rows.transpose(0, 2, 1)),
        "pixels": split_table(pixels),
        "pixels_back": split_table(pixels.T),
        "spread": split_table3(spread),
        "spread_back": split_table(spread.T),
    }


def split(value):
    high = value.astype(BF16)
    low = (value - high.astype(F32)).astype(BF16)
    return high, low


def dot(former, latter):
    return lax.dot_general(
        former, latter, (((1,), (0,)), ((), ())), preferred_element_type=F32
    )


def dot_last(former, latter):
    return lax.dot_general(
        former, latter, (((1,), (1,)), ((), ())), preferred_element_type=F32
    )


def dot3(former, latter, dot=dot):
    return (
        dot(former[0], latter[0]) + dot(former[0], latter[1]) + dot(former[1], latter[0])
    )


def dot3_deep(former, latter):
    twice = jnp.concatenate([former[0], former[0]], 1)
    return dot(twice, jnp.concatenate(latter, 0)) + dot(former[1], latter[0])


def dot6(former, latter):
    high, mid = split(former)
    low = ((former - high.astype(F32)) - mid.astype(F32)).astype(BF16)
    count = former.shape[0]
    most = dot(jnp.concatenate([high, mid, low], 0), latter[0])
    some = dot(jnp.concatenate([high, mid], 0), latter[1])
    small = dot(high, latter[2]) + some[count:] + most[2 * count :]
    return small + some[:count] + most[count : 2 * count] + most[:count]


def pair(ref):
    return ref[0], ref[1]


def moved(flip, value):
    high, low = split(value)
    return dot(flip, high) + dot(flip, low)


def moved_right(value, flip):
    high, low = split(value)
    return dot(high, flip) + dot(low, flip)


def pair_up(value):
    return jnp.concatenate([value[:HALF], value[ROOM : ROOM + HALF]], 1)


def alternate(shape):
    return 1.0 - 2.0 * (lax.broadcasted_iota(jnp.int32, shape, 0) % 2).astype(F32)


def weight_kernel(weight_ref, out_ref):
    row = lax.broadcasted_iota(jnp.int32, out_ref.shape, 0)
    out_ref[...] = jnp.where(row == WEIGHT_ROW - HALF + 8, weight_ref[0], weight_ref[1])


def neighbours(outer, inner):
    tile = lax.axis_index("tile")
    last = lax.axis_size("tile") - 1
    outer = jnp.where((tile > 0) & (tile < last), outer, 0.0)
    odd = tile % 2 == 1
    return jnp.where(odd, inner, outer), jnp.where(odd, outer, inner)


def window_kernel(outer_ref, inner_ref, mask_ref, rows_ref, heavy_ref, out_ref):
    above, below = neighbours(outer_ref[...], inner_ref[...])
    above, below = above[:, TILE - HALO :], below[:, :HALO]
    sides = jnp.concatenate([below, above], 1)
    both = split(jnp.concatenate([mask_ref[...], sides], 0))
    done = dot3(pair(rows_ref), both, dot_last)
    own, halo = done[:, :SHARD], done[:, SHARD:]
    done = pair_up(own) + alternate((HALF, 2 * SHARD)) * pair_up(halo)
    row = lax.broadcasted_iota(jnp.int32, (8, 2 * SHARD), 0) + HALF - 8
    out_ref[: HALF - 8] = done[: HALF - 8]
    out_ref[HALF - 8 :] = jnp.where(row < WEIGHT_ROW, done[HALF - 8 :], heavy_ref[...])


def padded(row):
    return jnp.concatenate([row, jnp.zeros((1, FREQS - HALF), F32)], 1)


def with_edges(value, edges, weights=None):
    row = lax.broadcasted_iota(jnp.int32, value.shape, 0)
    for slot, edge in enumerate(edges):
        value = jnp.where(row == EDGE_ROW + slot, padded(edge), value)
    if weights is None:
        return value
    heavy = jnp.concatenate([value[: HALF - 8], weights, value[HALF:]], 0)
    return jnp.where((row >= WEIGHT_ROW) & (row < HALF), heavy, value)


def edge_columns(value):
    columns = value[HALF - 8 : HALF].T[:HALF]
    first = EDGE_ROW - (HALF - 8)
    return jnp.concatenate([columns[:, first : first + 1], columns[:, first + 1 : first + 2]], 0)


def band_kernel(r0, r1, r2, r3, band_ref, out_ref):
    kern = lax.axis_index("kern")
    at_y, at_z = kern // 4, kern % 4
    blocks = [ref[...] for ref in (r0, r1, r2, r3)]
    cos = jnp.concatenate([block[:, :SHARD] for block in blocks], 1)
    sin = jnp.concatenate([block[:, SHARD:] for block in blocks], 1)
    places = [4 * at_y + (at_z ^ step) for step in range(4)]
    band = tuple(
        jnp.concatenate([band_ref[i, pl.ds(place, 1)][0] for place in places], 0)
        for i in range(2)
    )
    done = dot3(split(jnp.concatenate([cos, sin], 0)), band)
    edges = [done[half : half + HALF, FREQS:].T[:1] for half in (0, HALF)]
    out_ref[...] = with_edges(done[:, :FREQS], edges, r0[HALF - 8 :])


def aerial_kernel(
    p0, p1, p2, p3, h0, h1, h2, h3, unfold_ref, flip_ref, out_rows_ref, pixels_ref,
    field_ref, image_ref,
):
    at_y = lax.axis_index("kern") // 4
    total = (p0[...] + p1[...]) + (p2[...] + p3[...])
    done = moved_right(total, unfold_ref[...])
    lane = lax.broadcasted_iota(jnp.int32, done.shape, 1)
    done = jnp.where(lane == FREQS, edge_columns(total), done)
    cos_cos, cos_sin = done[:HALF, :FREQS], done[:HALF, FREQS:]
    sin_cos, sin_sin = done[HALF:, :FREQS], done[HALF:, FREQS:]
    plus = jnp.concatenate([cos_cos - sin_sin, -(cos_sin + sin_cos)], 1)
    minus = jnp.concatenate([cos_cos + sin_sin, sin_cos - cos_sin], 1)
    spectrum = jnp.concatenate([moved(flip_ref[...], minus), plus[: FREQS // 2]], 0)
    spec_re, spec_im = spectrum[:, :FREQS], spectrum[:, FREQS:]
    out_rows = (
        out_rows_ref[0, pl.ds(at_y, 1)][0],
        out_rows_ref[1, pl.ds(at_y, 1)][0],
    )
    mids = []
    weights = []
    for part_ref, kernel_ref in zip((p0, p1, p2, p3), (h0, h1, h2, h3)):
        for slot in range(2):
            kern_re, kern_im = kernel_ref[slot, 0], kernel_ref[slot, 1]
            row = WEIGHT_ROW + slot
            weights.append(part_ref[row : row + 1, :1])
            band = jnp.concatenate(
                [
                    kern_re * spec_re - kern_im * spec_im,
                    kern_re * spec_im + kern_im * spec_re,
                ],
                1,
            )
            quads = dot3_deep(out_rows, split(band))
            upper, lower = quads[:QUARTER], quads[QUARTER:]
            mids.append(
                jnp.concatenate(
                    [
                        upper[:, :FREQS] - lower[:, FREQS:],
                        upper[:, FREQS:] + lower[:, :FREQS],
                    ],
                    1,
                )
            )
    field = dot3(split(jnp.concatenate(mids, 0)), pair(pixels_ref))
    image = None
    for slot in range(COUNT):
        part = field[slot * QUARTER : (slot + 1) * QUARTER]
        heavy = part * weights[slot]
        field_ref[slot * QUARTER : (slot + 1) * QUARTER, :] = heavy
        part = part * heavy
        part = part[:, :SAMPLES] + part[:, SAMPLES:]
        image = part if image is None else image + part
    image_ref[...] = image


def slope_kernel(
    i0, i1, i2, i3, goal_ref, field_ref, h0, h1, h2, h3,
    spread_ref, spread_back_ref, pixels_back_ref, out_back_ref, flip_back_ref,
    fold_ref, m0, m1, m2, m3, resist_ref,
):
    kern = lax.axis_index("kern")
    at_y, at_z = kern // 4, kern % 4
    image = (i0[...] + i1[...]) + (i2[...] + i3[...])
    image = dot6(image, spread_ref)
    resist = 1.0 / (1.0 + jnp.exp(-STEEPNESS * (image - THRESHOLD)))
    goal = goal_ref[...].astype(F32)
    slope = 2.0 * STEEPNESS * (resist - goal) * resist * (1.0 - resist)
    slope = slope.astype(BF16)
    slope = dot(slope, spread_back_ref[0]) + dot(slope, spread_back_ref[1])
    slope = jnp.concatenate([slope, slope], 1)
    freqs = []
    for first in range(0, COUNT, 2):
        weighted = jnp.concatenate(
            [
                slope * field_ref[slot * QUARTER : (slot + 1) * QUARTER, :]
                for slot in range(first, first + 2)
            ],
            0,
        )
        freqs.append(dot3(split(weighted), pair(pixels_back_ref)))
    freqs = jnp.concatenate(freqs, 0)
    out_back = (
        out_back_ref[0, pl.ds(at_y, 1)][0],
        out_back_ref[1, pl.ds(at_y, 1)][0],
    )
    grad_re = grad_im = None
    for slot in range(COUNT):
        kernel_ref = (h0, h1, h2, h3)[slot // 2]
        kern_re, kern_im = kernel_ref[slot % 2, 0], kernel_ref[slot % 2, 1]
        part = freqs[slot * QUARTER : (slot + 1) * QUARTER]
        block = jnp.concatenate(
            [part, jnp.concatenate([part[:, FREQS:], -part[:, :FREQS]], 1)], 0
        )
        adjoint = dot3_deep(out_back, split(block))
        adj_re, adj_im = adjoint[:, :FREQS], adjoint[:, FREQS:]
        term_re = kern_re * adj_re + kern_im * adj_im
        term_im = kern_re * adj_im - kern_im * adj_re
        grad_re = term_re if grad_re is None else grad_re + term_re
        grad_im = term_im if grad_im is None else grad_im + term_im
    grad = jnp.concatenate([grad_re, grad_im], 1)
    plus = jnp.concatenate(
        [grad[FREQS // 2 :], jnp.zeros((HALF - FREQS // 2, 2 * FREQS), F32)], 0
    )
    minus = moved(flip_back_ref[...], grad[: FREQS // 2])
    both, less = plus + minus, minus - plus
    done = jnp.concatenate(
        [
            jnp.concatenate([both[:, :FREQS], -both[:, FREQS:]], 1),
            jnp.concatenate([less[:, FREQS:], less[:, :FREQS]], 1),
        ],
        0,
    )
    first = done[:, FREQS : FREQS + 8].T[:1]
    done = moved_right(done, fold_ref[...])
    done = with_edges(done, (first[:, :HALF], first[:, HALF:]))
    resist_ref[...] = resist
    for step, message in enumerate((m0, m1, m2, m3)):
        message[: 2 * HALF, :] = done
        block = 4 * (at_y ^ step) + at_z
        start = pl.multiple_of((block // 2) * 2 * SHARD, 2 * SHARD)
        wide = resist_ref[:, pl.ds(start, 2 * SHARD)].T
        piece = jnp.where(block % 2 == 0, wide[:SHARD], wide[SHARD:])
        message[2 * HALF :, :] = jnp.concatenate([piece[:EXTRA], piece[EXTRA:]], 1)


def columns_kernel(
    m0, m1, m2, m3, band_back_ref, edge_ref, g0, g1, g2, g3, order_ref
):
    kern = lax.axis_index("kern")
    at_y, at_z = kern // 4, kern % 4
    rows = slice(0, 2 * HALF)
    total = (m0[rows] + m1[rows]) + (m2[rows] + m3[rows])
    start = pl.multiple_of(at_y * WIDE, WIDE)
    band = tuple(band_back_ref[i, :, pl.ds(start, WIDE)] for i in range(2))
    done = dot3(split(total), band)
    done = done + edge_columns(total) * edge_ref[:1, pl.ds(start, WIDE)]
    for slot in range(4):
        cols = slice(slot * SHARD, (slot + 1) * SHARD)
        order_ref[slot] = jnp.concatenate([done[:HALF, cols], done[HALF:, cols]], 1)
    for step, out in enumerate((g0, g1, g2, g3)):
        out[...] = order_ref[pl.ds(at_z ^ step, 1)][0]


def resist_kernel(m0, m1, m2, m3, resist_ref):
    at_y = lax.axis_index("kern") // 4
    pieces = []
    for message in (m0, m1, m2, m3):
        piece = message[2 * HALF :, :]
        pieces.append(jnp.concatenate([piece[:, :SHARD], piece[:, SHARD:]], 0))
    spots = []
    for slot in range(4):
        spot = pieces[0]
        for step in (1, 2, 3):
            spot = jnp.where((at_y ^ step) == slot, pieces[step], spot)
        spots.append(spot)
    resist_ref[...] = jnp.concatenate(spots, 1)


def final_kernel(inner_ref, outer_ref, own_ref, rows_ref, out_ref):
    above, below = neighbours(outer_ref[...], inner_ref[...])
    own = own_ref[...]
    sign = 2.0 * alternate(own.shape)
    own = 2.0 * own
    sides = (
        own + above * sign,
        own + below * sign,
    )
    for slot, side in enumerate(sides):
        side = split(jnp.concatenate([side, jnp.zeros((ROOM - HALF, 2 * SHARD), F32)], 0).T)
        cols = slice(slot * HALO, (slot + 1) * HALO)
        total = None
        for half in range(2):
            part = dot3(
                (side[0][half * SHARD : (half + 1) * SHARD], side[1][half * SHARD : (half + 1) * SHARD]),
                tuple(rows_ref[i, half * ROOM : (half + 1) * ROOM, cols] for i in range(2)),
            )
            total = part if total is None else total + part
        out_ref[:, cols] = total


def call(kernel, shapes, *operands, flops=4 * 10**9, smem=(), hbm=(), scratch=()):
    many = isinstance(shapes, list)
    space = lambda i: pltpu.SMEM if i in smem else pltpu.HBM if i in hbm else pltpu.VMEM
    spec = lambda i: pl.BlockSpec(memory_space=space(i))
    out = [jax.ShapeDtypeStruct(shape, F32) for shape in (shapes if many else [shapes])]
    return pl.pallas_call(
        kernel,
        scratch_shapes=list(scratch),
        out_shape=out if many else out[0],
        in_specs=[spec(i) for i in range(len(operands))],
        out_specs=[pl.BlockSpec(memory_space=pltpu.VMEM)] * len(out)
        if many
        else pl.BlockSpec(memory_space=pltpu.VMEM),
        compiler_params=pltpu.CompilerParams(vmem_limit_bytes=32 * 2**20),
        cost_estimate=pl.CostEstimate(flops=flops, bytes_accessed=10**6, transcendentals=0),
        name=kernel.__name__,
    )(*operands)


def swap_y(value, step):
    return lax.ppermute(value, "kern", [(i, i ^ (4 * step)) for i in range(16)])


def swap_z(value, step):
    return lax.ppermute(value, "kern", [(i, i ^ step) for i in range(16)])


def swap_inner(value):
    return lax.ppermute(value, "tile", [(i, i ^ 1) for i in range(16)])


def swap_outer(value):
    return lax.ppermute(value, "tile", [(i, ((i + 1) ^ 1) - 1 & 15) for i in range(16)])


def per_device(mask_field, target, kernel_spectra, kernel_weight):
    table = {name: jnp.asarray(value) for name, value in tables().items()}
    at_y = lax.axis_index("kern") // 4
    order = [pltpu.VMEM((4, HALF, 2 * SHARD), F32)]
    mask_field = mask_field.T
    inner, outer = swap_inner(mask_field), swap_outer(mask_field)
    heavy = call(weight_kernel, (8, 2 * SHARD), kernel_weight, smem=(0,))
    kernel_spectra, heavy = lax.optimization_barrier((kernel_spectra, heavy))
    kernels = [kernel_spectra] + [swap_y(kernel_spectra, step) for step in (1, 2, 3)]

    rows = call(
        window_kernel, (HALF, 2 * SHARD), outer, inner, mask_field, table["rows"], heavy
    )
    rows = [rows] + [swap_z(rows, step) for step in (1, 2, 3)]
    *rows, h1, h3 = lax.optimization_barrier((*rows, kernels[1], kernels[3]))
    kernels = [kernel_spectra, h1, kernels[2], h3]
    part = call(
        band_kernel, (2 * HALF, FREQS), *rows, table["band"]
    )
    near, far, middle = [swap_y(part, step) for step in (1, 3, 2)]
    parts = [part, near, middle, far]
    field, image = call(
        aerial_kernel,
        [(COUNT * QUARTER, 2 * SAMPLES), (QUARTER, SAMPLES)],
        *parts, *kernels, table["unfold"], table["flip"], table["out"],
        table["pixels"], flops=4 * 10**9,
    )
    images = [image] + [swap_z(image, step) for step in (1, 3, 2)]
    goal = lax.dynamic_slice_in_dim(target, at_y * QUARTER, QUARTER, 0)
    messages = call(
        slope_kernel,
        [(2 * HALF + EXTRA, FREQS)] * 4,
        *images, goal, field, *kernels, table["spread"], table["spread_back"],
        table["pixels_back"], table["out_back"], table["flip_back"], table["fold"],
        scratch=[pltpu.VMEM((QUARTER, COLS), F32)],
    )
    messages = [messages[0]] + [swap_y(messages[step], step) for step in (1, 2, 3)]
    resist = call(resist_kernel, (SHARD, TILE), *messages)
    grads = call(
        columns_kernel,
        [(HALF, 2 * SHARD)] * 4,
        *messages, table["band_back"], table["edge_back"], scratch=order,
    )
    near, middle, far = [swap_z(grads[step], step) for step in (1, 2, 3)]
    near, resist = lax.optimization_barrier((near, resist))
    grad = (grads[0] + near) + (middle + far)
    mask_grad = call(
        final_kernel, (SHARD, TILE), swap_inner(grad), swap_outer(grad), grad,
        table["rows"],
    )
    return (resist.T, mask_grad.T)


def solution(mesh):
    in_specs = (P("tile", "kern"), P("tile", None), P("kern", None, None, None), P("kern"))
    out_specs = (P("tile", "kern"), P("tile", "kern"))
    return jax.shard_map(
        per_device, mesh=mesh, in_specs=in_specs, out_specs=out_specs, check_vma=False
    )
```

```python
import math

import jax
import jax.numpy as jnp
import ml_dtypes
import numpy as np
from jax import lax
from jax.experimental import pallas as pl
from jax.experimental.pallas import tpu as pltpu
from jax.sharding import PartitionSpec as P

COLS = 1024
HALO = 128
FREQS = 128
TILE = 256
WINDOW = 512
SHARD = 64
SAMPLES = 256
QUARTER = 64
COUNT = 8
HALF = 72
ROOM = 80
EDGE_ROW = 65
WEIGHT_ROW = 67
EXTRA = 32
WIDE = 4 * SHARD
STEEPNESS = 4.0
THRESHOLD = 1.0
F32 = jnp.float32
BF16 = jnp.bfloat16


def angles(places, frequencies, length):
    return (np.outer(places, frequencies) % length) * (2.0 * math.pi / length)


def split_table(value):
    value = value.astype(np.float32)
    high = value.astype(ml_dtypes.bfloat16)
    low = (value - high.astype(np.float32)).astype(ml_dtypes.bfloat16)
    return np.stack([high, low])


def split_table3(value):
    pair = split_table(value)
    rest = value - pair.astype(np.float64).sum(0)
    return np.concatenate([pair, rest.astype(ml_dtypes.bfloat16)[None]])


def tables():
    freq = np.arange(FREQS) - FREQS // 2
    scale = 1.0 / math.sqrt(WINDOW * COLS)
    win = angles(np.arange(FREQS // 2 + 1), HALO + np.arange(TILE), WINDOW)
    rows = np.zeros((2, ROOM, TILE))
    rows[0, : FREQS // 2 + 1] = np.cos(win) * scale
    rows[1, : FREQS // 2 + 1] = np.sin(win) * scale
    rows = rows.reshape(2 * ROOM, TILE)
    col = angles(np.arange(COLS), freq, COLS)
    keep = FREQS // 2
    band = np.concatenate([np.cos(col[:, keep:]), np.sin(col[:, keep:])], 1)
    band[:, keep] = np.cos(col[:, 0])
    edge = np.sin(col[:, 0])
    wide = np.zeros((COLS // SHARD, SHARD, 2 * FREQS))
    wide[:, :, :FREQS] = band.reshape(COLS // SHARD, SHARD, FREQS)
    wide[:, :, FREQS] = edge.reshape(COLS // SHARD, SHARD)
    unfold = np.zeros((FREQS, 2 * FREQS))
    for place, value in enumerate(freq):
        size = abs(value)
        unfold[size, place] = 1.0
        if 0 < size < keep:
            unfold[keep + size, FREQS + place] = np.sign(value)
    flip = np.zeros((FREQS // 2, HALF))
    flip[np.arange(FREQS // 2), FREQS // 2 - np.arange(FREQS // 2)] = 1.0
    out = angles(HALO + np.arange(TILE), freq, WINDOW).reshape(4, QUARTER, FREQS)
    out_rows = np.concatenate([np.cos(out), np.sin(out)], 1) / FREQS
    pix = angles(freq, np.arange(SAMPLES), SAMPLES)
    pix_cos, pix_sin = np.cos(pix), np.sin(pix)
    pixels = np.concatenate(
        [np.concatenate([pix_cos, pix_sin], 1), np.concatenate([-pix_sin, pix_cos], 1)], 0
    )
    gap = np.arange(COLS)[None, :] - (COLS // SAMPLES) * np.arange(SAMPLES)[:, None]
    waves = np.arange(1, SAMPLES // 2)
    base = 2.0 * math.pi / COLS
    line = (1.0 + 2.0 * np.cos(base * np.outer(np.arange(COLS), waves)).sum(1)) / SAMPLES
    spread = line[gap % COLS]
    return {
        "rows": split_table(rows),
        "band": split_table(wide),
        "band_back": split_table(band.T),
        "edge_back": np.tile(edge, (8, 1)).astype(np.float32),
        "unfold": unfold.astype(ml_dtypes.bfloat16),
        "fold": unfold.T.astype(ml_dtypes.bfloat16),
        "flip": flip.astype(ml_dtypes.bfloat16),
        "flip_back": flip.T.astype(ml_dtypes.bfloat16),
        "out": split_table(out_rows),
        "out_back": split_table(out_rows.transpose(0, 2, 1)),
        "pixels": split_table(pixels),
        "pixels_back": split_table(pixels.T),
        "spread": split_table3(spread),
        "spread_back": split_table(spread.T),
    }


def split(value):
    high = value.astype(BF16)
    low = (value - high.astype(F32)).astype(BF16)
    return high, low


def dot(former, latter):
    return lax.dot_general(
        former, latter, (((1,), (0,)), ((), ())), preferred_element_type=F32
    )


def dot_last(former, latter):
    return lax.dot_general(
        former, latter, (((1,), (1,)), ((), ())), preferred_element_type=F32
    )


def dot3(former, latter, dot=dot):
    return (
        dot(former[0], latter[0]) + dot(former[0], latter[1]) + dot(former[1], latter[0])
    )


def dot3_deep(former, latter):
    twice = jnp.concatenate([former[0], former[0]], 1)
    return dot(twice, jnp.concatenate(latter, 0)) + dot(former[1], latter[0])


def dot6(former, latter):
    high, mid = split(former)
    low = ((former - high.astype(F32)) - mid.astype(F32)).astype(BF16)
    count = former.shape[0]
    most = dot(jnp.concatenate([high, mid, low], 0), latter[0])
    some = dot(jnp.concatenate([high, mid], 0), latter[1])
    small = dot(high, latter[2]) + some[count:] + most[2 * count :]
    return small + some[:count] + most[count : 2 * count] + most[:count]


def pair(ref):
    return ref[0], ref[1]


def moved(flip, value):
    high, low = split(value)
    return dot(flip, high) + dot(flip, low)


def moved_right(value, flip):
    high, low = split(value)
    return dot(high, flip) + dot(low, flip)


def pair_up(value):
    return jnp.concatenate([value[:HALF], value[ROOM : ROOM + HALF]], 1)


def alternate(shape):
    return 1.0 - 2.0 * (lax.broadcasted_iota(jnp.int32, shape, 0) % 2).astype(F32)


def weight_kernel(weight_ref, out_ref):
    row = lax.broadcasted_iota(jnp.int32, out_ref.shape, 0)
    out_ref[...] = jnp.where(row == WEIGHT_ROW - HALF + 8, weight_ref[0], weight_ref[1])


def neighbours(outer, inner):
    tile = lax.axis_index("tile")
    last = lax.axis_size("tile") - 1
    outer = jnp.where((tile > 0) & (tile < last), outer, 0.0)
    odd = tile % 2 == 1
    return jnp.where(odd, inner, outer), jnp.where(odd, outer, inner)


def window_kernel(outer_ref, inner_ref, mask_ref, rows_ref, heavy_ref, out_ref):
    above, below = neighbours(outer_ref[...], inner_ref[...])
    above, below = above[:, TILE - HALO :], below[:, :HALO]
    sides = jnp.concatenate([below, above], 1)
    both = split(jnp.concatenate([mask_ref[...], sides], 0))
    done = dot3(pair(rows_ref), both, dot_last)
    own, halo = done[:, :SHARD], done[:, SHARD:]
    done = pair_up(own) + alternate((HALF, 2 * SHARD)) * pair_up(halo)
    row = lax.broadcasted_iota(jnp.int32, (8, 2 * SHARD), 0) + HALF - 8
    out_ref[: HALF - 8] = done[: HALF - 8]
    out_ref[HALF - 8 :] = jnp.where(row < WEIGHT_ROW, done[HALF - 8 :], heavy_ref[...])


def padded(row):
    return jnp.concatenate([row, jnp.zeros((1, FREQS - HALF), F32)], 1)


def with_edges(value, edges, weights=None):
    row = lax.broadcasted_iota(jnp.int32, value.shape, 0)
    for slot, edge in enumerate(edges):
        value = jnp.where(row == EDGE_ROW + slot, padded(edge), value)
    if weights is None:
        return value
    heavy = jnp.concatenate([value[: HALF - 8], weights, value[HALF:]], 0)
    return jnp.where((row >= WEIGHT_ROW) & (row < HALF), heavy, value)


def edge_columns(value):
    columns = value[HALF - 8 : HALF].T[:HALF]
    first = EDGE_ROW - (HALF - 8)
    return jnp.concatenate([columns[:, first : first + 1], columns[:, first + 1 : first + 2]], 0)


def band_kernel(r0, r1, r2, r3, band_ref, out_ref):
    kern = lax.axis_index("kern")
    at_y, at_z = kern // 4, kern % 4
    blocks = [ref[...] for ref in (r0, r1, r2, r3)]
    cos = jnp.concatenate([block[:, :SHARD] for block in blocks], 1)
    sin = jnp.concatenate([block[:, SHARD:] for block in blocks], 1)
    places = [4 * at_y + (at_z ^ step) for step in range(4)]
    band = tuple(
        jnp.concatenate([band_ref[i, pl.ds(place, 1)][0] for place in places], 0)
        for i in range(2)
    )
    done = dot3(split(jnp.concatenate([cos, sin], 0)), band)
    edges = [done[half : half + HALF, FREQS:].T[:1] for half in (0, HALF)]
    out_ref[...] = with_edges(done[:, :FREQS], edges, r0[HALF - 8 :])


def aerial_kernel(
    p0, p1, p2, p3, h0, h1, h2, h3, unfold_ref, flip_ref, out_rows_ref, pixels_ref,
    field_ref, image_ref,
):
    at_y = lax.axis_index("kern") // 4
    total = (p0[...] + p1[...]) + (p2[...] + p3[...])
    done = moved_right(total, unfold_ref[...])
    lane = lax.broadcasted_iota(jnp.int32, done.shape, 1)
    done = jnp.where(lane == FREQS, edge_columns(total), done)
    cos_cos, cos_sin = done[:HALF, :FREQS], done[:HALF, FREQS:]
    sin_cos, sin_sin = done[HALF:, :FREQS], done[HALF:, FREQS:]
    plus = jnp.concatenate([cos_cos - sin_sin, -(cos_sin + sin_cos)], 1)
    minus = jnp.concatenate([cos_cos + sin_sin, sin_cos - cos_sin], 1)
    spectrum = jnp.concatenate([moved(flip_ref[...], minus), plus[: FREQS // 2]], 0)
    spec_re, spec_im = spectrum[:, :FREQS], spectrum[:, FREQS:]
    out_rows = (
        out_rows_ref[0, pl.ds(at_y, 1)][0],
        out_rows_ref[1, pl.ds(at_y, 1)][0],
    )
    mids = []
    weights = []
    for part_ref, kernel_ref in zip((p0, p1, p2, p3), (h0, h1, h2, h3)):
        for slot in range(2):
            kern_re, kern_im = kernel_ref[slot, 0], kernel_ref[slot, 1]
            row = WEIGHT_ROW + slot
            weights.append(part_ref[row : row + 1, :1])
            band = jnp.concatenate(
                [
                    kern_re * spec_re - kern_im * spec_im,
                    kern_re * spec_im + kern_im * spec_re,
                ],
                1,
            )
            quads = dot3_deep(out_rows, split(band))
            upper, lower = quads[:QUARTER], quads[QUARTER:]
            mids.append(
                jnp.concatenate(
                    [
                        upper[:, :FREQS] - lower[:, FREQS:],
                        upper[:, FREQS:] + lower[:, :FREQS],
                    ],
                    1,
                )
            )
    field = dot3(split(jnp.concatenate(mids, 0)), pair(pixels_ref))
    image = None
    for slot in range(COUNT):
        part = field[slot * QUARTER : (slot + 1) * QUARTER]
        heavy = part * weights[slot]
        field_ref[slot * QUARTER : (slot + 1) * QUARTER, :] = heavy
        part = part * heavy
        part = part[:, :SAMPLES] + part[:, SAMPLES:]
        image = part if image is None else image + part
    image_ref[...] = image


def slope_kernel(
    i0, i1, i2, i3, goal_ref, field_ref, h0, h1, h2, h3,
    spread_ref, spread_back_ref, pixels_back_ref, out_back_ref, flip_back_ref,
    fold_ref, m0, m1, m2, m3, resist_ref,
):
    kern = lax.axis_index("kern")
    at_y, at_z = kern // 4, kern % 4
    image = (i0[...] + i1[...]) + (i2[...] + i3[...])
    image = dot6(image, spread_ref)
    resist = 1.0 / (1.0 + jnp.exp(-STEEPNESS * (image - THRESHOLD)))
    goal = goal_ref[...].astype(F32)
    slope = 2.0 * STEEPNESS * (resist - goal) * resist * (1.0 - resist)
    slope = slope.astype(BF16)
    slope = dot(slope, spread_back_ref[0]) + dot(slope, spread_back_ref[1])
    slope = jnp.concatenate([slope, slope], 1)
    freqs = []
    for first in range(0, COUNT, 2):
        weighted = jnp.concatenate(
            [
                slope * field_ref[slot * QUARTER : (slot + 1) * QUARTER, :]
                for slot in range(first, first + 2)
            ],
            0,
        )
        freqs.append(dot3(split(weighted), pair(pixels_back_ref)))
    freqs = jnp.concatenate(freqs, 0)
    out_back = (
        out_back_ref[0, pl.ds(at_y, 1)][0],
        out_back_ref[1, pl.ds(at_y, 1)][0],
    )
    grad_re = grad_im = None
    for slot in range(COUNT):
        kernel_ref = (h0, h1, h2, h3)[slot // 2]
        kern_re, kern_im = kernel_ref[slot % 2, 0], kernel_ref[slot % 2, 1]
        part = freqs[slot * QUARTER : (slot + 1) * QUARTER]
        block = jnp.concatenate(
            [part, jnp.concatenate([part[:, FREQS:], -part[:, :FREQS]], 1)], 0
        )
        adjoint = dot3_deep(out_back, split(block))
        adj_re, adj_im = adjoint[:, :FREQS], adjoint[:, FREQS:]
        term_re = kern_re * adj_re + kern_im * adj_im
        term_im = kern_re * adj_im - kern_im * adj_re
        grad_re = term_re if grad_re is None else grad_re + term_re
        grad_im = term_im if grad_im is None else grad_im + term_im
    grad = jnp.concatenate([grad_re, grad_im], 1)
    plus = jnp.concatenate(
        [grad[FREQS // 2 :], jnp.zeros((HALF - FREQS // 2, 2 * FREQS), F32)], 0
    )
    minus = moved(flip_back_ref[...], grad[: FREQS // 2])
    both, less = plus + minus, minus - plus
    done = jnp.concatenate(
        [
            jnp.concatenate([both[:, :FREQS], -both[:, FREQS:]], 1),
            jnp.concatenate([less[:, FREQS:], less[:, :FREQS]], 1),
        ],
        0,
    )
    first = done[:, FREQS : FREQS + 8].T[:1]
    done = moved_right(done, fold_ref[...])
    done = with_edges(done, (first[:, :HALF], first[:, HALF:]))
    resist_ref[...] = resist
    for step, message in enumerate((m0, m1, m2, m3)):
        message[: 2 * HALF, :] = done
        block = 4 * (at_y ^ step) + at_z
        start = pl.multiple_of((block // 2) * 2 * SHARD, 2 * SHARD)
        wide = resist_ref[:, pl.ds(start, 2 * SHARD)].T
        piece = jnp.where(block % 2 == 0, wide[:SHARD], wide[SHARD:])
        message[2 * HALF :, :] = jnp.concatenate([piece[:EXTRA], piece[EXTRA:]], 1)


def columns_kernel(
    m0, m1, m2, m3, band_back_ref, edge_ref, g0, g1, g2, g3, order_ref
):
    kern = lax.axis_index("kern")
    at_y, at_z = kern // 4, kern % 4
    rows = slice(0, 2 * HALF)
    total = (m0[rows] + m1[rows]) + (m2[rows] + m3[rows])
    start = pl.multiple_of(at_y * WIDE, WIDE)
    band = tuple(band_back_ref[i, :, pl.ds(start, WIDE)] for i in range(2))
    done = dot3(split(total), band)
    done = done + edge_columns(total) * edge_ref[:1, pl.ds(start, WIDE)]
    for slot in range(4):
        cols = slice(slot * SHARD, (slot + 1) * SHARD)
        order_ref[slot] = jnp.concatenate([done[:HALF, cols], done[HALF:, cols]], 1)
    for step, out in enumerate((g0, g1, g2, g3)):
        out[...] = order_ref[pl.ds(at_z ^ step, 1)][0]


def resist_kernel(m0, m1, m2, m3, resist_ref):
    at_y = lax.axis_index("kern") // 4
    pieces = []
    for message in (m0, m1, m2, m3):
        piece = message[2 * HALF :, :]
        pieces.append(jnp.concatenate([piece[:, :SHARD], piece[:, SHARD:]], 0))
    spots = []
    for slot in range(4):
        spot = pieces[0]
        for step in (1, 2, 3):
            spot = jnp.where((at_y ^ step) == slot, pieces[step], spot)
        spots.append(spot)
    resist_ref[...] = jnp.concatenate(spots, 1)


def final_kernel(inner_ref, outer_ref, own_ref, rows_ref, out_hbm, out_ref, sems):
    above, below = neighbours(outer_ref[...], inner_ref[...])
    own = own_ref[...]
    sign = 2.0 * alternate(own.shape)
    own = 2.0 * own
    sides = (
        own + above * sign,
        own + below * sign,
    )
    copies = []
    for slot, side in enumerate(sides):
        side = split(jnp.concatenate([side, jnp.zeros((ROOM - HALF, 2 * SHARD), F32)], 0).T)
        cols = slice(slot * HALO, (slot + 1) * HALO)
        total = None
        for half in range(2):
            part = dot3(
                (side[0][half * SHARD : (half + 1) * SHARD], side[1][half * SHARD : (half + 1) * SHARD]),
                tuple(rows_ref[i, half * ROOM : (half + 1) * ROOM, cols] for i in range(2)),
            )
            total = part if total is None else total + part
        out_ref[slot] = total
        copies.append(
            pltpu.make_async_copy(out_ref.at[slot], out_hbm.at[:, cols], sems.at[slot])
        )
        copies[-1].start()
    for copy in copies:
        copy.wait()


def call(
    kernel, shapes, *operands, flops=4 * 10**9, smem=(), hbm=(), scratch=(), out_space=pltpu.VMEM
):
    many = isinstance(shapes, list)
    space = lambda i: pltpu.SMEM if i in smem else pltpu.HBM if i in hbm else pltpu.VMEM
    spec = lambda i: pl.BlockSpec(memory_space=space(i))
    out = [jax.ShapeDtypeStruct(shape, F32) for shape in (shapes if many else [shapes])]
    return pl.pallas_call(
        kernel,
        scratch_shapes=list(scratch),
        out_shape=out if many else out[0],
        in_specs=[spec(i) for i in range(len(operands))],
        out_specs=[pl.BlockSpec(memory_space=pltpu.VMEM)] * len(out)
        if many
        else pl.BlockSpec(memory_space=out_space),
        compiler_params=pltpu.CompilerParams(vmem_limit_bytes=32 * 2**20),
        cost_estimate=pl.CostEstimate(flops=flops, bytes_accessed=10**6, transcendentals=0),
        name=kernel.__name__,
    )(*operands)


def swap_y(value, step):
    return lax.ppermute(value, "kern", [(i, i ^ (4 * step)) for i in range(16)])


def swap_z(value, step):
    return lax.ppermute(value, "kern", [(i, i ^ step) for i in range(16)])


def swap_inner(value):
    return lax.ppermute(value, "tile", [(i, i ^ 1) for i in range(16)])


def swap_outer(value):
    return lax.ppermute(value, "tile", [(i, ((i + 1) ^ 1) - 1 & 15) for i in range(16)])


def per_device(mask_field, target, kernel_spectra, kernel_weight):
    table = {name: jnp.asarray(value) for name, value in tables().items()}
    at_y = lax.axis_index("kern") // 4
    order = [pltpu.VMEM((4, HALF, 2 * SHARD), F32)]
    mask_field = mask_field.T
    inner, outer = swap_inner(mask_field), swap_outer(mask_field)
    heavy = call(weight_kernel, (8, 2 * SHARD), kernel_weight, smem=(0,))
    kernel_spectra, heavy = lax.optimization_barrier((kernel_spectra, heavy))
    kernels = [kernel_spectra] + [swap_y(kernel_spectra, step) for step in (1, 2, 3)]

    rows = call(
        window_kernel, (HALF, 2 * SHARD), outer, inner, mask_field, table["rows"], heavy
    )
    rows = [rows] + [swap_z(rows, step) for step in (1, 2, 3)]
    *rows, h1, h3 = lax.optimization_barrier((*rows, kernels[1], kernels[3]))
    kernels = [kernel_spectra, h1, kernels[2], h3]
    part = call(
        band_kernel, (2 * HALF, FREQS), *rows, table["band"]
    )
    near, far, middle = [swap_y(part, step) for step in (1, 3, 2)]
    parts = [part, near, middle, far]
    field, image = call(
        aerial_kernel,
        [(COUNT * QUARTER, 2 * SAMPLES), (QUARTER, SAMPLES)],
        *parts, *kernels, table["unfold"], table["flip"], table["out"],
        table["pixels"], flops=4 * 10**9,
    )
    images = [image] + [swap_z(image, step) for step in (1, 3, 2)]
    goal = lax.dynamic_slice_in_dim(target, at_y * QUARTER, QUARTER, 0)
    messages = call(
        slope_kernel,
        [(2 * HALF + EXTRA, FREQS)] * 4,
        *images, goal, field, *kernels, table["spread"], table["spread_back"],
        table["pixels_back"], table["out_back"], table["flip_back"], table["fold"],
        scratch=[pltpu.VMEM((QUARTER, COLS), F32)],
    )
    messages = [messages[0]] + [swap_y(messages[step], step) for step in (1, 2, 3)]
    resist = call(resist_kernel, (SHARD, TILE), *messages)
    grads = call(
        columns_kernel,
        [(HALF, 2 * SHARD)] * 4,
        *messages, table["band_back"], table["edge_back"], scratch=order,
    )
    near, middle, far = [swap_z(grads[step], step) for step in (1, 2, 3)]
    near, resist = lax.optimization_barrier((near, resist))
    grad = (grads[0] + near) + (middle + far)
    mask_grad = call(
        final_kernel, (SHARD, TILE), swap_inner(grad), swap_outer(grad), grad,
        table["rows"],
        scratch=[pltpu.VMEM((2, SHARD, HALO), F32), pltpu.SemaphoreType.DMA((2,))],
        out_space=pltpu.HBM,
    )
    return (resist.T, mask_grad.T)


def solution(mesh):
    in_specs = (P("tile", "kern"), P("tile", None), P("kern", None, None, None), P("kern"))
    out_specs = (P("tile", "kern"), P("tile", "kern"))
    return jax.shard_map(
        per_device, mesh=mesh, in_specs=in_specs, out_specs=out_specs, check_vma=False
    )
```
